256 devices in a mesh: tile: 32 (over x, y, core), mem: 8 (over z).
Axes of the slice: x: 4, y: 4, z: 8, core: 2. Of those that a mesh axis runs over, the one named last changes fastest.
Arguments:
- members: bfloat16 [80, 4, 512, 512], P('mem', None, 'tile'), may hold values from -6 to 6
- weights: bfloat16 [65536, 128], P('tile'), may hold values from -0.5 to 0.5
- modes_in: float32 [4, 65536], P(None, 'tile'), may hold values from -120 to 120
- obs_tile: int32 [65536, 1], P('tile'), may hold values from 0 to 31; in each aligned block of 2048 rows (0 to 2047, 2048 to 4095, ...) at most 128 rows name the same one
- obs_block: int32 [65536], P('tile'), may hold values from 0 to 255
Outputs:
- modes_out: float32 [4, 65536], P(None, 'tile')
- eigen: float32 [4], replicated
The draws below stay inside these ranges and needn't reach their ends.
Inputs may be any that keep to these rules, and one draw needn't show every extreme that they name: Among the observations of one tile, at most 128 name the same tile in obs_tile, a bound that some block reaches by one tile's observations.
All inputs are finite; a program needn't handle non-finite values.
Results may differ from the reference program's by a relative error of at most 0.0032.
Values may be sent and summed in bfloat16 or wider, within the bound.
No kernel may reach another device: no remote copies, remote signals or barrier semaphores. Data moves between devices by JAX's collectives and lax.ppermute only.
A program may use at most 128 MiB of HBM per device.

```python
import math
import jax
import jax.numpy as jnp
import numpy as np
from jax import lax

CX = 16
NY = 512
LEV = 4
BX = 4
BY = 8
K = 4
STEPS = 4
OBS_DEV = 2048
WB = 128
CAP = 128
NX = 512
NOBS = 65536
MEMBERS = 80
BLK_TILE = 256
N_TILE = 32


def draw_modes_in(key, part):
    key_base = jax.random.fold_in(key, 11)
    key_scale = jax.random.fold_in(key, 12)
    position = jnp.arange(NOBS, dtype=jnp.float32) / max(NOBS - 1, 1)
    rising = 1.0 + 2.0 * position
    scale_row = jnp.exp(jnp.log(10.0) * jax.random.uniform(key_scale, (NOBS,), jnp.float32))
    values = jnp.clip(jax.random.normal(key_base, (K, NOBS), jnp.float32), -4.0, 4.0)
    return (values * (scale_row * rising)[None, :]).astype(jnp.float32)


def plant(entries, own_key, low, largest):
    extent = entries.shape
    place = [jax.random.randint(jax.random.fold_in(own_key, axis), (), 0, extent[axis]) for axis in range(len(extent))]
    entries = entries.at[tuple(place)].set(low)
    longest = extent.index(max(extent))
    place[longest] = (place[longest] + 1) % extent[longest]
    return entries.at[tuple(place)].set(largest)


def shard_levels(rng, dims, split, smallest, largest):
    def one(dim, blocks):
        draws = jax.random.uniform(jax.random.fold_in(jax.random.fold_in(rng, 6), dim), (blocks,), jnp.float32, smallest / len(split), largest / len(split))
        return jnp.repeat(jnp.exp(draws), dims[dim] // blocks).reshape((-1,) + (1,) * (len(dims) - dim - 1))

    gain = one(*split[0])
    for cut in split[1:]:
        gain = gain * one(*cut)
    return gain


def assign_block(key, own, number, rows, count, top, bound, slope):
    sequence = jax.random.permutation(key, count)
    heavy_load, usual = portions_of(count, rows * top, bound, slope, True), portions_of(count, rows * top, bound, slope, False)
    places = jnp.arange(count)

    def named(sizes, offset_by):
        used = int((sizes > 0).sum())
        fixed = max(1, used // 4)
        shifted = fixed + (places - fixed + offset_by * (used - fixed)) % max(1, count - fixed)
        return jnp.zeros((count,), jnp.int32).at[sequence[jnp.where(places < fixed, places, shifted)]].set(jnp.asarray(sizes, jnp.int32))

    sizes = jnp.where(number % 4 == 0, named(heavy_load, number // 4), named(usual, number - number // 4 - 1))
    mixed = jax.random.permutation(jax.random.fold_in(own, 3), count)
    giver, sink = mixed[0:count // 2 * 2:2], mixed[1:count // 2 * 2:2]
    slack = jnp.minimum(sizes[giver] - 1, bound - sizes[sink]) // 2
    slack = jnp.where((giver == sequence[0]) | (sink == sequence[0]) | (sizes[sink] == 0), 0, jnp.maximum(slack, 0))
    shifted = jax.random.randint(jax.random.fold_in(own, 4), (count // 2,), 0, 1 << 20) % (slack + 1)
    sizes = sizes.at[giver].add(-shifted).at[sink].add(shifted)
    items = jnp.searchsorted(jnp.cumsum(sizes), jnp.arange(rows * top), side="right").astype(jnp.int32)
    listing = items.reshape(top, rows).T
    listing = listing[jax.random.permutation(jax.random.fold_in(own, 1), rows)]
    offset_by = jax.random.randint(jax.random.fold_in(own, 2), (rows, 1), 0, top)
    return jnp.take_along_axis(listing, (jnp.arange(top)[None, :] + offset_by) % top, axis=1)


def portions_of(amount, total, limit, lean, full):
    loads = [(1 << 20) // math.isqrt(rank ** lean) + 1 for rank in range(1, amount + 1)]
    largest = limit if full else min(limit, max(-(-total // amount), total * loads[0] // sum(loads)))
    least = 1 if total - largest >= amount - 1 else 0
    counts, surplus = [largest] + [least] * (amount - 1), total - largest - least * (amount - 1)
    while surplus > 0:
        candidates = [i for i in range(1, amount) if counts[i] < largest] or [i for i in range(1, amount) if counts[i] < limit]
        pool, left = sum([loads[i] for i in candidates]), surplus
        for i in candidates:
            more = min(limit - counts[i], max(1, left * loads[i] // pool), surplus)
            counts[i] = counts[i] + more
            surplus = surplus - more
    return np.array(counts)


def noise(key, shape, scale, reach, pieces=(), kind=jnp.bfloat16):
    gain = shard_levels(key, shape, pieces, -0.22, 0.18) if pieces else 1.0
    values = jax.random.normal(key, shape, jnp.float32) * scale * gain
    return jnp.minimum(jnp.maximum(values, -reach), reach).astype(kind)


def setup_inputs(seed: int = 0) -> dict:
    key_list = jax.random.split(jax.random.key(seed), 6)
    members = noise(key_list[0], (MEMBERS, LEV, NX, NY), 1.0, 6.0, ((0, 8), (2, 32)))
    weights = noise(key_list[1], (NOBS, WB), WB ** -0.5, 0.5, ((0, 32),))
    modes_in = draw_modes_in(jax.random.fold_in(key_list[5], 71), 0)
    obs_tile_keys = jax.random.split(jax.random.fold_in(key_list[3], 1), NOBS // OBS_DEV)
    obs_tile_turns = jax.random.permutation(jax.random.fold_in(key_list[3], 3), NOBS // OBS_DEV)
    obs_tile = jax.vmap(lambda own, number: assign_block(jax.random.fold_in(key_list[3], 2), own, number, OBS_DEV, N_TILE, 1, CAP, 2))(obs_tile_keys, obs_tile_turns).reshape((NOBS, 1))
    obs_block = plant(jax.random.randint(key_list[4], (NOBS,), 0, BLK_TILE), jax.random.fold_in(key_list[4], 1), 0, BLK_TILE - 1).astype(jnp.int32)
    return dict(members=members, weights=weights, modes_in=modes_in, obs_tile=obs_tile, obs_block=obs_block)


diffusion_rate = 0.2

def smooth_core(center, left_side, right_side):
    padded = jnp.pad(center, [(0, 0)] * (center.ndim - 1) + [(1, 1)], mode='edge')
    return center + diffusion_rate * (left_side + right_side + (padded[..., :-2] + padded[..., 2:]) - 4.0 * center)

def reference(members, weights, modes_in, obs_tile, obs_block):
    blocks_x = CX // BX
    blocks_y = NY // BY
    modes_half = modes_in.astype(jnp.bfloat16)
    weights_f = weights.astype(jnp.float32)
    contrib = (weights_f[:, None, :] * modes_half.T.astype(jnp.float32)[:, :, None]).astype(jnp.bfloat16)
    global_block = (obs_tile[:, 0] * BLK_TILE + obs_block).astype(jnp.int32)
    summed = jax.ops.segment_sum(contrib.astype(jnp.float32).reshape(NOBS, K * WB), global_block, num_segments=N_TILE * BLK_TILE)
    spread = summed.reshape(N_TILE, blocks_x, blocks_y, K, LEV, BX, BY).transpose(3, 4, 0, 1, 5, 2, 6).reshape(K, LEV, NX, NY)

    def member_term(running, member):
        member_f = member.astype(jnp.float32)[None]
        action = member_f * spread
        for sweep_index in range(STEPS):
            action = smooth_core(action, jnp.roll(action, 1, axis=-2), jnp.roll(action, -1, axis=-2))
        return (running + member_f * action, None)
    summed_image, unused = lax.scan(member_term, jnp.zeros((K, LEV, NX, NY), jnp.float32), members)
    covariance_image = summed_image / (MEMBERS - 1)
    image_blocks = covariance_image.reshape(K, LEV, N_TILE, blocks_x, BX, blocks_y, BY).transpose(2, 3, 5, 0, 1, 4, 6).reshape(N_TILE * BLK_TILE, K, WB)
    picked = image_blocks[global_block]
    images = jnp.sum(weights_f[:, None, :] * picked, axis=2).T
    gram = jnp.dot(images.astype(jnp.float32), images.T.astype(jnp.float32), precision=lax.Precision.HIGHEST, preferred_element_type=jnp.float32) / NOBS
    lower = jnp.linalg.cholesky(gram)
    modes_out = jax.scipy.linalg.solve_triangular(lower, images, lower=True)
    eigen = jnp.sum(modes_in * images, axis=1) / jnp.sum(modes_in * modes_in, axis=1)
    return (modes_out, eigen)
```

```python
import functools

import jax
import jax.numpy as jnp
from jax import lax
from jax.experimental import pallas as pl
from jax.experimental.pallas import tpu as pltpu
from jax.sharding import PartitionSpec as P

BX = 4
BY = 8
STEPS = 4
MODES = 4
ROWS = 80
TAIL = 64
HALO = 4
F32 = jnp.float32
BF16 = jnp.bfloat16


def stencil_points():
    counts = {(0, 0): 1}
    for _ in range(STEPS):
        wider = {}
        for (dx, dy), n in counts.items():
            for sx, sy in ((0, 0), (1, 0), (-1, 0), (0, 1), (0, -1)):
                key = (dx + sx, dy + sy)
                wider[key] = wider.get(key, 0) + n
        counts = wider
    return sorted((dx, dy, n) for (dx, dy), n in counts.items())


POINTS = stencil_points()
TOTAL = float(5**STEPS)

NT = (((1,), (1,)), ((), ()))
NN = (((1,), (0,)), ((), ()))


def matmul(a, b, dims):
    return lax.dot_general(a, b, dims, preferred_element_type=F32)


def iota(shape, dim):
    return lax.broadcasted_iota(jnp.int32, shape, dim)


def vmem(limit=40):
    return pltpu.CompilerParams(vmem_limit_bytes=limit << 20)


def pack_kernel(half_ref, w_ref, modes_ref, dest_ref, block_ref, out_ref, hot_ref, x_ref, tail_ref, xm_ref):
    n_tiles = out_ref.shape[0]
    obs = w_ref.shape[0]
    half = half_ref[0]
    q = iota((TAIL, 128), 0)
    source = (2 * half + (q >> 5)) * 32 + (q & 3) * 8 + ((q >> 2) & 7)
    order = jnp.where(iota((TAIL, 128), 1) == source, 1.0, 0.0).astype(BF16)
    x_ref[0:TAIL, :] = matmul(order, w_ref[...], NT).astype(BF16)
    m = modes_ref[...]
    hi = m.astype(BF16).astype(F32)
    mid = (m - hi).astype(BF16).astype(F32)
    lo = (m - hi) - mid
    tail_ref[0:4, :] = hi
    tail_ref[4:8, :] = mid
    tail_ref[8:12, :] = lo
    tail_ref[12:13, :] = (block_ref[...] + 1).astype(F32)
    tail_ref[13:16, :] = jnp.zeros((3, obs), F32)
    x_ref[TAIL:ROWS, :] = tail_ref[...].astype(BF16)
    chunk = 256
    upper = jnp.where(iota((chunk, chunk), 0) < iota((chunk, chunk), 1), 1.0, 0.0).astype(BF16)
    off = jnp.zeros((n_tiles, 1), F32)
    for c in range(obs // chunk):
        at = slice(c * chunk, (c + 1) * chunk)
        d = jnp.where(iota((n_tiles, chunk), 0) == dest_ref[:, at], 1.0, 0.0)
        before = matmul(d.astype(BF16), upper, NN) + off
        rank = jnp.sum(d * before, axis=0, keepdims=True).astype(jnp.int32)
        hot_ref[:, at] = jnp.where(iota((128, chunk), 0) == rank, 1.0, 0.0).astype(BF16)
        off = off + jnp.sum(d, axis=1, keepdims=True)
    group = 8
    for g in range(n_tiles // group):
        for t in range(group):
            here = jnp.where(dest_ref[...] == g * group + t, 1.0, 0.0)
            here = jnp.broadcast_to(here, (16, obs)).astype(BF16)
            for r in range(ROWS // 16):
                row = g * group * ROWS + t * ROWS + r * 16
                xm_ref[row : row + 16, :] = x_ref[r * 16 : r * 16 + 16, :] * here
        rows = group * ROWS
        sent = matmul(xm_ref[g * rows : (g + 1) * rows, :], hot_ref[...], NT)
        out_ref[g * group : (g + 1) * group] = sent.astype(BF16).reshape(group, ROWS, 128)


def extend(ext_ref, lead):
    lane = iota((ext_ref.shape[-2], 128), 1) & 63
    for n in range(HALO):
        low = pltpu.roll(ext_ref[lead, HALO + BY - HALO + n], 1, 1)
        ext_ref[lead, n] = jnp.where(lane == 0, ext_ref[lead, HALO + HALO - 1 - n], low)
        high = pltpu.roll(ext_ref[lead, HALO + n], 127, 1)
        ext_ref[lead, HALO + BY + n] = jnp.where(lane == 63, ext_ref[lead, HALO + BY - 1 - n], high)


def pair_kernel(scale, keep_ref, got_ref, low_ref, high_ref, out_ref, ext_ref):
    count = keep_ref.shape[0]
    total = 2 * count
    rows = keep_ref.shape[2]
    ny = keep_ref.shape[3]
    y = iota((ny, 128), 0)
    lane = iota((ny, 128), 1)
    for c in range(BY):
        low = jnp.where(y == (lane & 63) * BY + c, 1.0, 0.0)
        left = jnp.where(lane < 64, low, 0.0).astype(BF16)
        right = jnp.where(lane < 64, 0.0, low).astype(BF16)
        for part, ref in enumerate((keep_ref, got_ref)):
            r = matmul(ref[:, 0].reshape(count * rows, ny), left, NN) + matmul(
                ref[:, 1].reshape(count * rows, ny), right, NN
            )
            ext_ref[part * count : (part + 1) * count, HALO + c, HALO : HALO + rows, :] = r.reshape(
                count, rows, 128
            )
        for first, ref in ((0, low_ref), (HALO + rows, high_ref)):
            r = matmul(ref[0], left, NN) + matmul(ref[1], right, NN)
            for m in range(total):
                ext_ref[m, HALO + c, first : first + HALO, :] = r[m * HALO : (m + 1) * HALO, :]

    def widen(m, carry):
        extend(ext_ref, m)
        return carry

    lax.fori_loop(0, total, widen, 0)

    def plane(c, carry):
        for xv in range(rows // 8):

            def member(m, sums):
                here = ext_ref[m, HALO + c, HALO + xv * 8 : HALO + xv * 8 + 8, :]
                return tuple(
                    s + here * ext_ref[m, HALO + c + dy, HALO + xv * 8 + dx : HALO + xv * 8 + dx + 8, :]
                    for s, (dx, dy, n) in zip(sums, POINTS)
                )

            sums = lax.fori_loop(
                0, total, member, tuple(jnp.zeros((8, 128), F32) for _ in POINTS)
            )
            for i, (s, (dx, dy, n)) in enumerate(zip(sums, POINTS)):
                out_ref[i, c, xv * 8 : xv * 8 + 8, :] = s * (n * scale)
        return carry

    lax.fori_loop(0, BY, plane, 0)


def block_hot(tail):
    return jnp.where((iota((256, 128), 0) + 1).astype(F32) == tail[12:13, :], 1.0, 0.0).astype(BF16)


def spread_kernel(recv_ref, out_ref, low_ref, high_ref, g_ref, h_ref):
    n_tiles = recv_ref.shape[0]
    for s in range(n_tiles):
        at = slice(s * 128, (s + 1) * 128)
        w = recv_ref[s, 0:TAIL, :].astype(F32)
        tail = recv_ref[s, TAIL:ROWS, :].astype(F32)
        h_ref[:, at] = block_hot(tail)
        for l in range(2):
            for k in range(MODES):
                row = l * 128 + k * 32
                g_ref[row : row + 32, at] = (w[l * 32 : l * 32 + 32, :] * tail[k : k + 1, :]).astype(BF16)
    r = matmul(g_ref[...], h_ref[...], NT)
    for i in range(4):
        t = jnp.concatenate([r[0:128, i * 64 : i * 64 + 64], r[128:256, i * 64 : i * 64 + 64]], axis=1)
        if i == 0:
            low_ref[...] = t
        if i == 3:
            high_ref[...] = t
        for n in range(MODES * BY):
            out_ref[n, i * 4 : i * 4 + 4, :] = t[n * 4 : n * 4 + 4, :]


def image_kernel(recv_ref, f_ref, low_ref, high_ref, c_ref, out_ref, ext_ref, v_ref, t_ref, h_ref):
    n_tiles = recv_ref.shape[0]
    rows = f_ref.shape[1]
    for k in range(MODES):
        for c in range(BY):
            n = k * BY + c
            ext_ref[k, HALO + c, HALO : HALO + rows, :] = f_ref[n]
            ext_ref[k, HALO + c, 0:HALO, :] = low_ref[n * 4 : n * 4 + 4, :]
            ext_ref[k, HALO + c, HALO + rows : HALO + rows + HALO, :] = high_ref[n * 4 : n * 4 + 4, :]
        extend(ext_ref, k)

    def plane(c, carry):
        for xv in range(rows // 8):
            sums = [jnp.zeros((8, 128), F32) for _ in range(MODES)]
            for i, (dx, dy, n) in enumerate(POINTS):
                weight = c_ref[i, c, xv * 8 : xv * 8 + 8, :]
                first = HALO + xv * 8 + dx
                for k in range(MODES):
                    sums[k] = sums[k] + weight * ext_ref[k, HALO + c + dy, first : first + 8, :]
            for k in range(MODES):
                v_ref[k, c, xv * 8 : xv * 8 + 8, :] = sums[k]
        return carry

    lax.fori_loop(0, BY, plane, 0)
    for i in range(4):
        for k in range(MODES):
            for c in range(BY):
                n = k * BY + c
                t_ref[i, n * 4 : n * 4 + 4, :] = v_ref[k, c, i * 4 : i * 4 + 4, :]
    cov = jnp.concatenate(
        [
            jnp.concatenate([t_ref[i, :, l * 64 : l * 64 + 64] for i in range(4)], axis=1)
            for l in range(2)
        ],
        axis=0,
    )
    hi = cov.astype(BF16)
    lo = (cov - hi.astype(F32)).astype(BF16)
    both = jnp.concatenate([hi, lo], axis=0)
    for s in range(n_tiles):
        h_ref[:, s * 128 : (s + 1) * 128] = block_hot(recv_ref[s, TAIL:ROWS, :].astype(F32))
    group = 4
    cross = jnp.zeros((MODES, 128), F32)
    square = jnp.zeros((MODES, 128), F32)
    for g in range(n_tiles // group):
        picked = matmul(both, h_ref[:, g * group * 128 : (g + 1) * group * 128], NN)
        picked = picked[0:256] + picked[256:512]
        for j in range(group):
            s = g * group + j
            w = recv_ref[s, 0:TAIL, :].astype(F32)
            tail = recv_ref[s, TAIL:ROWS, :].astype(F32)
            first = (s % 2) * 4
            for k in range(MODES):
                part = picked[k * 32 : k * 32 + 32, j * 128 : (j + 1) * 128] * w[0:32]
                part = part + picked[128 + k * 32 : 160 + k * 32, j * 128 : (j + 1) * 128] * w[32:64]
                out_ref[0, s // 2, first + k : first + k + 1, :] = jnp.sum(part, axis=0, keepdims=True)
            mode = tail[0:4] + tail[4:8] + tail[8:12]
            cross = cross + mode * out_ref[0, s // 2, first : first + 4, :]
            square = square + mode * mode
    out_ref[0, n_tiles // 2, 0:4, :] = cross
    out_ref[0, n_tiles // 2, 4:8, :] = square * (1.0 / out_ref.shape[0])
    for m in range(1, out_ref.shape[0]):
        out_ref[m] = out_ref[0]


def gram_kernel(parts_ref, out_ref):
    n_tiles = out_ref.shape[0]
    groups = parts_ref.shape[0]
    pairs = n_tiles // 2
    sums = [jnp.zeros((8, 128), F32) for _ in range(MODES)]
    lane = iota((4, 128), 1)
    for p in range(pairs):
        z = parts_ref[0, p]
        for m in range(1, groups):
            z = z + parts_ref[m, p]
        out_ref[2 * p, 0:4, :] = z[0:4]
        out_ref[2 * p + 1, 0:4, :] = z[4:8]
        for d in range(MODES):
            sums[d] = sums[d] + z * (z if d == 0 else pltpu.roll(z, d, 0))
    last = parts_ref[0, pairs]
    for m in range(1, groups):
        last = last + parts_ref[m, pairs]
    stats = jnp.zeros((4, 128), F32)
    for d in range(MODES):
        both = sums[d][0:4] + sums[d][4:8]
        stats = jnp.where(lane == d, jnp.sum(both, axis=1, keepdims=True), stats)
    stats = jnp.where(lane == 4, jnp.sum(last[0:4], axis=1, keepdims=True), stats)
    stats = jnp.where(lane == 5, jnp.sum(last[4:8], axis=1, keepdims=True), stats)
    for s in range(n_tiles):
        out_ref[s, 4:8, :] = stats


def finish_kernel(back_ref, hot_ref, dest_ref, modes_ref, eigen_ref, split_ref):
    n_tiles = back_ref.shape[0]
    obs = dest_ref.shape[1]
    count = n_tiles * obs
    total = back_ref[0]
    for t in range(1, n_tiles):
        total = total + back_ref[t]

    def stat(k, lane):
        return total[4 + k : 5 + k, lane : lane + 1]

    def g(k, j):
        return stat(k, k - j) * (1.0 / count)

    low = {}
    for j in range(MODES):
        d = g(j, j)
        for p in range(j):
            d = d - low[j, p] * low[j, p]
        low[j, j] = jnp.sqrt(d)
        for k in range(j + 1, MODES):
            v = g(k, j)
            for p in range(j):
                v = v - low[k, p] * low[j, p]
            low[k, j] = v / low[j, j]
    a = back_ref[...].reshape(n_tiles * 8, 128)
    rows = n_tiles * 8
    hi = a.astype(BF16)
    rest = a - hi.astype(F32)
    mid = rest.astype(BF16)
    split_ref[0:rows, :] = hi
    split_ref[rows : 2 * rows, :] = mid
    split_ref[2 * rows : 3 * rows, :] = (rest - mid.astype(F32)).astype(BF16)
    chunk = 512
    for c in range(obs // chunk):
        at = slice(c * chunk, (c + 1) * chunk)
        r = matmul(split_ref[...], hot_ref[:, at], NN)
        r = (r[0:rows] + r[rows : 2 * rows]) + r[2 * rows : 3 * rows]
        dest = jnp.broadcast_to(dest_ref[:, at], (8, chunk))
        image = jnp.zeros((8, chunk), F32)
        for t in range(n_tiles):
            image = image + jnp.where(dest == t, r[t * 8 : t * 8 + 8], 0.0)
        done = []
        for k in range(MODES):
            v = image[k : k + 1]
            for p in range(k):
                v = v - low[k, p] * done[p]
            done.append(v / low[k, k])
            modes_ref[k : k + 1, at] = done[k]
    for k in range(MODES):
        eigen_ref[k : k + 1, :] = jnp.broadcast_to(stat(k, 4) / stat(k, 5), (1, 128))


VM = pl.BlockSpec(memory_space=pltpu.VMEM)
SM = pl.BlockSpec(memory_space=pltpu.SMEM)


def struct(shape, dtype):
    return jax.ShapeDtypeStruct(shape, dtype)


def on_device(members, weights, modes_in, obs_tile, obs_block):
    n_tiles = lax.axis_size("tile")
    n_groups = lax.axis_size("mem")
    obs, width = weights.shape
    count, levels, rows, ny = members.shape
    half = lax.axis_index("mem") % 2
    dest = obs_tile.reshape(1, obs)
    block = obs_block.reshape(1, obs)

    with jax.named_scope("pack"):
        sent, hot = pl.pallas_call(
            pack_kernel,
            in_specs=[SM, VM, VM, VM, VM],
            out_specs=[VM, VM],
            out_shape=[struct((n_tiles, ROWS, 128), BF16), struct((128, obs), BF16)],
            scratch_shapes=[
                pltpu.VMEM((ROWS, obs), BF16),
                pltpu.VMEM((16, obs), F32),
                pltpu.VMEM((n_tiles * ROWS, obs), BF16),
            ],
            compiler_params=vmem(),
        )(half.reshape(1), weights, modes_in, dest, block)
    with jax.named_scope("forward"):
        recv = lax.all_to_all(sent, "tile", 0, 0, tiled=True)

    with jax.named_scope("swap"):
        keep = lax.dynamic_slice_in_dim(members, 2 * half, 2, axis=1)
        give = lax.dynamic_slice_in_dim(members, 2 - 2 * half, 2, axis=1)
        got = lax.ppermute(give, "mem", [(m, m ^ 1) for m in range(n_groups)])
    up = [(t, (t + 1) % n_tiles) for t in range(n_tiles)]
    down = [(b, a) for a, b in up]

    def edge(first):
        both = jnp.concatenate([keep[:, :, first : first + HALO], got[:, :, first : first + HALO]], axis=0)
        return both.transpose(1, 0, 2, 3).reshape(2, 2 * count * HALO, ny)

    with jax.named_scope("member_edges"):
        m_low = lax.ppermute(edge(rows - HALO), "tile", up)
        m_high = lax.ppermute(edge(0), "tile", down)
    with jax.named_scope("pairs"):
        scale = 1.0 / (TOTAL * (count * n_groups - 1))
        pairs = pl.pallas_call(
            functools.partial(pair_kernel, scale),
            in_specs=[VM] * 4,
            out_specs=VM,
            out_shape=struct((len(POINTS), BY, rows, 128), F32),
            scratch_shapes=[pltpu.VMEM((2 * count, BY + 2 * HALO, rows + 2 * HALO, 128), F32)],
            compiler_params=vmem(),
        )(keep, got, m_low, m_high)

    with jax.named_scope("spread"):
        field, f_low, f_high = pl.pallas_call(
            spread_kernel,
            in_specs=[VM],
            out_specs=[VM] * 3,
            out_shape=[
                struct((MODES * BY, rows, 128), F32),
                struct((128, 128), F32),
                struct((128, 128), F32),
            ],
            scratch_shapes=[
                pltpu.VMEM((256, n_tiles * 128), BF16),
                pltpu.VMEM((256, n_tiles * 128), BF16),
            ],
            compiler_params=vmem(),
        )(recv)
    with jax.named_scope("spread_edges"):
        s_low = lax.ppermute(f_high, "tile", up)
        s_high = lax.ppermute(f_low, "tile", down)
    with jax.named_scope("images"):
        parts = pl.pallas_call(
            image_kernel,
            in_specs=[VM] * 5,
            out_specs=VM,
            out_shape=struct((n_groups, n_tiles // 2 + 1, 8, 128), F32),
            scratch_shapes=[
                pltpu.VMEM((MODES, BY + 2 * HALO, rows + 2 * HALO, 128), F32),
                pltpu.VMEM((MODES, BY, rows, 128), F32),
                pltpu.VMEM((4, 128, 128), F32),
                pltpu.VMEM((256, n_tiles * 128), BF16),
            ],
            compiler_params=vmem(),
        )(recv, field, s_low, s_high, pairs)
    with jax.named_scope("group_sum"):
        parts = lax.all_to_all(parts, "mem", 0, 0, tiled=True)
    with jax.named_scope("gram"):
        back = pl.pallas_call(
            gram_kernel,
            in_specs=[VM],
            out_specs=VM,
            out_shape=struct((n_tiles, 8, 128), F32),
        )(parts)
    with jax.named_scope("return"):
        back = lax.all_to_all(back, "tile", 0, 0, tiled=True)
    with jax.named_scope("finish"):
        modes_out, eigen = pl.pallas_call(
            finish_kernel,
            in_specs=[VM] * 3,
            out_specs=[VM] * 2,
            out_shape=[struct((MODES, obs), F32), struct((MODES, 128), F32)],
            scratch_shapes=[pltpu.VMEM((3 * n_tiles * 8, 128), BF16)],
            compiler_params=vmem(),
        )(back, hot, dest)
    return modes_out, eigen[:, 0]


def solution(mesh):
    in_specs = (
        P("mem", None, "tile", None),
        P("tile", None),
        P(None, "tile"),
        P("tile", None),
        P("tile"),
    )
    out_specs = (P(None, "tile"), P())
    return jax.shard_map(
        on_device, mesh=mesh, in_specs=in_specs, out_specs=out_specs, check_vma=False
    )
```

```python
import functools

import jax
import jax.numpy as jnp
from jax import lax
from jax.experimental import pallas as pl
from jax.experimental.pallas import tpu as pltpu
from jax.sharding import PartitionSpec as P

BX = 4
BY = 8
STEPS = 4
MODES = 4
ROWS = 80
TAIL = 64
HALO = 4
F32 = jnp.float32
BF16 = jnp.bfloat16


def stencil_points():
    counts = {(0, 0): 1}
    for _ in range(STEPS):
        wider = {}
        for (dx, dy), n in counts.items():
            for sx, sy in ((0, 0), (1, 0), (-1, 0), (0, 1), (0, -1)):
                key = (dx + sx, dy + sy)
                wider[key] = wider.get(key, 0) + n
        counts = wider
    return sorted((dx, dy, n) for (dx, dy), n in counts.items())


POINTS = [(dx, dy, n, i) for i, (dx, dy, n) in enumerate(stencil_points())]
EDGE_POINTS = [p for p in POINTS if p[0] > 0]
EDGE_POINTS = [(dx, dy, n, i) for i, (dx, dy, n, _) in enumerate(EDGE_POINTS)]
TOTAL = float(5**STEPS)

NT = (((1,), (1,)), ((), ()))
NN = (((1,), (0,)), ((), ()))


def matmul(a, b, dims):
    return lax.dot_general(a, b, dims, preferred_element_type=F32)


def iota(shape, dim):
    return lax.broadcasted_iota(jnp.int32, shape, dim)


def cost(us):
    return pl.CostEstimate(flops=0, bytes_accessed=us * 3_690_000, transcendentals=0)


def vmem(limit=16):
    return pltpu.CompilerParams(vmem_limit_bytes=limit << 20)


def pack_kernel(
    half_ref, w_any, modes_any, dest_any, block_any, members_any, out_ref, hot_ref, keep_ref,
    w_ref, modes_ref, dest_ref, block_ref, x_ref, tail_ref, xa_ref, xb_ref, sems,
):
    n_tiles = out_ref.shape[0]
    obs = w_ref.shape[0]
    half = half_ref[0]
    pairs = (
        (dest_any, dest_ref),
        (w_any, w_ref),
        (modes_any, modes_ref),
        (block_any, block_ref),
        (members_any.at[:, pl.ds(2 * half, 2)], keep_ref),
    )
    copies = [pltpu.make_async_copy(a, b, sems.at[i]) for i, (a, b) in enumerate(pairs)]
    for copy in copies:
        copy.start()
    copies[0].wait()
    chunk = 256
    upper = jnp.where(iota((chunk, chunk), 0) < iota((chunk, chunk), 1), 1.0, 0.0).astype(BF16)
    off = jnp.zeros((n_tiles, 1), F32)
    for c in range(obs // chunk):
        at = slice(c * chunk, (c + 1) * chunk)
        d = jnp.where(iota((n_tiles, chunk), 0) == dest_ref[:, at], 1.0, 0.0)
        before = matmul(d.astype(BF16), upper, NN) + off
        rank = jnp.sum(d * before, axis=0, keepdims=True).astype(jnp.int32)
        hot_ref[:, at] = jnp.where(iota((128, chunk), 0) == rank, 1.0, 0.0).astype(BF16)
        off = off + jnp.sum(d, axis=1, keepdims=True)
    for copy in copies[1:]:
        copy.wait()
    q = iota((TAIL, 128), 0)
    source = (2 * half + (q >> 5)) * 32 + (q & 3) * 8 + ((q >> 2) & 7)
    order = jnp.where(iota((TAIL, 128), 1) == source, 1.0, 0.0).astype(BF16)
    x_ref[0:TAIL, :] = matmul(order, w_ref[...], NT).astype(BF16)
    m = modes_ref[...]
    hi = m.astype(BF16).astype(F32)
    mid = (m - hi).astype(BF16).astype(F32)
    lo = (m - hi) - mid
    tail_ref[0:4, :] = hi
    tail_ref[4:8, :] = mid
    tail_ref[8:12, :] = lo
    tail_ref[12:13, :] = (block_ref[...] + 1).astype(F32)
    tail_ref[13:16, :] = jnp.zeros((3, obs), F32)
    x_ref[TAIL:ROWS, :] = tail_ref[...].astype(BF16)
    group = 8
    rows = group * ROWS

    def send(g, carry):
        for part, xm_ref in enumerate((xa_ref, xb_ref)):
            first = (2 * g + part) * group
            for t in range(group):
                here = jnp.where(dest_ref[...] == first + t, 1.0, 0.0)
                here = jnp.broadcast_to(here, (16, obs)).astype(BF16)
                for r in range(ROWS // 16):
                    row = t * ROWS + r * 16
                    xm_ref[row : row + 16, :] = x_ref[r * 16 : r * 16 + 16, :] * here
            sent = matmul(xm_ref[...], hot_ref[...], NT)
            out_ref[pl.ds(first, group)] = sent.astype(BF16).reshape(group, ROWS, 128)
        return carry

    lax.fori_loop(0, n_tiles // (2 * group), send, 0)


def extend(ext_ref, lead):
    lane = iota((ext_ref.shape[-2], 128), 1) & 63
    for n in range(HALO):
        low = pltpu.roll(ext_ref[lead, HALO + BY - HALO + n], 1, 1)
        ext_ref[lead, n] = jnp.where(lane == 0, ext_ref[lead, HALO + HALO - 1 - n], low)
        high = pltpu.roll(ext_ref[lead, HALO + n], 127, 1)
        ext_ref[lead, HALO + BY + n] = jnp.where(lane == 63, ext_ref[lead, HALO + BY - 1 - n], high)


def spread_rows(x, move):
    return matmul(x, move, NN)


def mover(ny):
    lane = iota((ny, ny), 1)
    return jnp.where(iota((ny, ny), 0) == (lane & 63) * BY + (lane >> 6), 1.0, 0.0).astype(BF16)


def join(first, second, p):
    a = first[:, p * 128 : (p + 1) * 128]
    b = second[:, p * 128 : (p + 1) * 128]
    left = iota(a.shape, 1) < 64
    return jnp.where(left, a, pltpu.roll(b, 64, 1)), jnp.where(left, pltpu.roll(a, 64, 1), b)


def pair_sums(center_of, ext_ref, out_ref, scale, c, at, points):
    total = ext_ref.shape[0]

    def member(m, sums):
        ext = {dy: ext_ref[m, HALO + c + dy, at : at + 8, :] for _, dy, _, _ in points}
        center = {dx: center_of(m, dx) for dx, _, _, _ in points}
        return tuple(s + center[dx] * ext[dy] for s, (dx, dy, _, _) in zip(sums, points))

    sums = lax.fori_loop(
        0, total, member, tuple(jnp.zeros((8, 128), F32) for _ in points), unroll=4
    )
    for s, (dx, dy, n, i) in zip(sums, points):
        out_ref[i, c, at : at + 8, :] = s * (n * scale)


def pair_kernel(scale, keep_ref, got_ref, out_ref, ends_ref, center_ref, ext_ref, y_ref):
    count = got_ref.shape[0]
    total = 2 * count
    rows = got_ref.shape[2]
    ny = got_ref.shape[3]
    move = mover(ny)
    side = count * 2 * rows
    y_ref[0:side, :] = spread_rows(keep_ref[...].reshape(side, ny), move)
    y_ref[side : 2 * side, :] = spread_rows(got_ref[...].reshape(side, ny), move)

    def place(m, carry):
        row = pl.multiple_of(m * 2 * rows, 2 * rows)
        first = y_ref[pl.ds(row, rows), :]
        second = y_ref[pl.ds(row + rows, rows), :]
        zero = jnp.zeros((8, 128), F32)
        for p in range(BY // 2):
            both = join(first, second, p)
            ends = [both[0][rows - HALO :], both[0][0:HALO], both[1][rows - HALO :], both[1][0:HALO]]
            ends_ref[m, p] = jnp.concatenate(ends, axis=0).astype(BF16)
            for i, v in enumerate(both):
                c = 2 * p + i
                ext_ref[m, HALO + c] = v
                center_ref[m, c, 0:8, :] = zero
                center_ref[m, c, 8 : 8 + rows, :] = v
                center_ref[m, c, 8 + rows : 16 + rows, :] = zero
        extend(ext_ref, m)
        return carry

    lax.fori_loop(0, total, place, 0, unroll=4)

    def plane(c, carry):
        for v in range(rows // 8):

            def center_of(m, dx):
                return center_ref[m, c, 8 + v * 8 - dx : 16 + v * 8 - dx, :]

            pair_sums(center_of, ext_ref, out_ref, scale, c, v * 8, POINTS)
        return carry

    lax.fori_loop(0, BY, plane, 0)


def pair_edge_kernel(scale, ends_ref, low_ref, high_ref, after_ref, out_ref, center_ref, ext_ref, y_ref):
    total = center_ref.shape[0]
    ny = low_ref.shape[2]
    side = 2 * total * HALO
    move = mover(ny)
    y_ref[0:side, :] = spread_rows(high_ref[...].reshape(side, ny), move)
    y_ref[side : 2 * side, :] = spread_rows(low_ref[...].reshape(side, ny), move)

    def place(m, carry):
        blocks = []
        for start in (0, side):
            row = pl.multiple_of(start + m * 2 * HALO, 8)
            blocks.append((y_ref[pl.ds(row, 8), :], y_ref[pl.ds(row + side // 2, 8), :]))
        top = iota((8, 128), 0) < HALO
        for p in range(BY // 2):
            for i, (high, low) in enumerate(zip(join(*blocks[0], p), join(*blocks[1], p))):
                ext_ref[2 * m, HALO + 2 * p + i] = jnp.where(top, high, pltpu.roll(low, HALO, 0))
                ext_ref[2 * m + 1, HALO + 2 * p + i] = jnp.where(top, pltpu.roll(high, HALO, 0), low)
        extend(ext_ref, 2 * m)
        extend(ext_ref, 2 * m + 1)
        for n in range(2):
            for p in range(BY // 2):
                ends = ends_ref[2 * m + n, p].astype(F32)
                for i in range(2):
                    center_ref[2 * m + n, 2 * p + i, 0:HALO, :] = ends[8 * i : 8 * i + HALO]
                    center_ref[2 * m + n, 2 * p + i, HALO : HALO + 8, :] = jnp.zeros((8, 128), F32)
                    center_ref[2 * m + n, 2 * p + i, HALO + 8 :, :] = ends[8 * i + HALO : 8 * i + 8]
        return carry

    lax.fori_loop(0, total // 2, place, 0, unroll=2)

    def plane(c, carry):
        def center_of(m, dx):
            return center_ref[m, c, HALO - dx : HALO + 8 - dx, :] + center_ref[m, c, HALO + dx : HALO + 8 + dx, :]

        pair_sums(center_of, ext_ref, out_ref, scale, c, 0, EDGE_POINTS)
        return carry

    lax.fori_loop(0, BY, plane, 0)


def block_hot(tail):
    return jnp.where((iota((256, 128), 0) + 1).astype(F32) == tail[12:13, :], 1.0, 0.0).astype(BF16)


def spread_kernel(recv_ref, after_ref, out_ref, low_ref, high_ref, g_ref, h_ref):
    n_tiles = recv_ref.shape[0]

    group = 8

    def sources(g, total):
        for j in range(group):
            at = slice(j * 128, (j + 1) * 128)
            w = recv_ref[g * group + j, 0:TAIL, :].astype(F32)
            tail = recv_ref[g * group + j, TAIL:ROWS, :].astype(F32)
            h_ref[:, at] = block_hot(tail)
            for l in range(2):
                for k in range(MODES):
                    row = l * 128 + k * 32
                    g_ref[row : row + 32, at] = (w[l * 32 : l * 32 + 32, :] * tail[k : k + 1, :]).astype(BF16)
        return total + matmul(g_ref[...], h_ref[...], NT)

    r = lax.fori_loop(0, n_tiles // group, sources, jnp.zeros((256, 256), F32))
    for i in range(4):
        t = jnp.concatenate([r[0:128, i * 64 : i * 64 + 64], r[128:256, i * 64 : i * 64 + 64]], axis=1)
        if i == 0:
            low_ref[...] = t
        if i == 3:
            high_ref[...] = t
        for n in range(MODES * BY):
            out_ref[n, i * 4 : i * 4 + 4, :] = t[n * 4 : n * 4 + 4, :]


def image_kernel(recv_ref, f_ref, low_ref, high_ref, c_ref, ce_ref, out_ref, ext_ref, side_ref, q_ref, t_ref):
    n_tiles = recv_ref.shape[0]
    rows = f_ref.shape[1]
    for k in range(MODES):
        for c in range(BY):
            n = k * BY + c
            ext_ref[k, HALO + c] = f_ref[n]
            side_ref[k, HALO + c, 0:HALO, :] = high_ref[n * 4 : n * 4 + 4, :]
            side_ref[k, HALO + c, HALO:8, :] = low_ref[n * 4 : n * 4 + 4, :]
        extend(ext_ref, k)
        extend(side_ref, k)

    def weigh(ref, v, c, points, weights):
        sums = [{} for _ in range(MODES)]
        for dx, dy, n, i in points:
            weight = weights[i, c, v * 8 : v * 8 + 8, :]
            for k in range(MODES):
                term = weight * ref[k, HALO + c + dy, v * 8 : v * 8 + 8, :]
                sums[k][dx] = sums[k][dx] + term if dx in sums[k] else term
        return sums

    def plane(cp, carry):
        for j in range(2):
            c = 2 * cp + j
            for v in range(rows // 8):
                for k, sums in enumerate(weigh(ext_ref, v, c, POINTS, c_ref)):
                    for dx, q in sums.items():
                        q_ref[k, j, dx + HALO, 8 + v * 8 : 16 + v * 8, :] = q
            for k, sums in enumerate(weigh(side_ref, 0, c, EDGE_POINTS, ce_ref)):
                for dx, q in sums.items():
                    q_ref[k, j, HALO - dx, 0:8, :] = q
                    q_ref[k, j, HALO + dx, rows + 8 : rows + 16, :] = q
        for k in range(MODES):
            for i in range(4):
                both = []
                for j in range(2):
                    at = 8 + i * 4
                    v = q_ref[k, j, HALO, at : at + 4, :]
                    for dx in range(-HALO, HALO + 1):
                        if dx != 0:
                            v = v + q_ref[k, j, dx + HALO, at + dx : at + dx + 4, :]
                    both.append(v)
                row = pl.multiple_of(k * 32 + cp * 8, 8)
                t_ref[i, pl.ds(row, 8), :] = jnp.concatenate(both, axis=0)
        return carry

    lax.fori_loop(0, BY // 2, plane, 0)
    cov = jnp.concatenate(
        [
            jnp.concatenate([t_ref[i, :, l * 64 : l * 64 + 64] for i in range(4)], axis=1)
            for l in range(2)
        ],
        axis=0,
    )
    hi = cov.astype(BF16)
    lo = (cov - hi.astype(F32)).astype(BF16)
    both = jnp.concatenate([hi, lo], axis=0)
    group = 8

    def image(g, carry):
        cross, square = carry
        hots = [block_hot(recv_ref[g * group + j, TAIL:ROWS, :].astype(F32)) for j in range(group)]
        picked = matmul(both, jnp.concatenate(hots, axis=1), NN)
        picked = picked[0:256] + picked[256:512]
        for j in range(group):
            s = g * group + j
            w = recv_ref[s, 0:TAIL, :].astype(F32)
            tail = recv_ref[s, TAIL:ROWS, :].astype(F32)
            first = (j % 2) * 4
            pair = g * (group // 2) + j // 2
            for k in range(MODES):
                part = picked[k * 32 : k * 32 + 32, j * 128 : (j + 1) * 128] * w[0:32]
                part = part + picked[128 + k * 32 : 160 + k * 32, j * 128 : (j + 1) * 128] * w[32:64]
                out_ref[pair, first + k : first + k + 1, :] = jnp.sum(part, axis=0, keepdims=True)
            mode = tail[0:4] + tail[4:8] + tail[8:12]
            cross = cross + mode * out_ref[pair, first : first + 4, :]
            square = square + mode * mode
        return cross, square

    zero = jnp.zeros((MODES, 128), F32)
    cross, square = lax.fori_loop(0, n_tiles // group, image, (zero, zero))
    out_ref[n_tiles // 2, 0:4, :] = cross
    out_ref[n_tiles // 2, 4:8, :] = square


def gram_kernel(groups, parts_ref, other_ref, out_ref):
    n_tiles = out_ref.shape[0]
    pairs = n_tiles // 2
    sums = [jnp.zeros((8, 128), F32) for _ in range(MODES)]
    lane = iota((4, 128), 1)
    for p in range(pairs):
        z = parts_ref[p] + other_ref[p]
        out_ref[2 * p, 0:4, :] = z[0:4]
        out_ref[2 * p + 1, 0:4, :] = z[4:8]
        for d in range(MODES):
            sums[d] = sums[d] + z * (z if d == 0 else pltpu.roll(z, d, 0))
    last = parts_ref[pairs] + other_ref[pairs]
    stats = jnp.zeros((4, 128), F32)
    for d in range(MODES):
        both = sums[d][0:4] + sums[d][4:8]
        stats = jnp.where(lane == d, jnp.sum(both, axis=1, keepdims=True), stats)
    stats = jnp.where(lane == 4, jnp.sum(last[0:4], axis=1, keepdims=True), stats)
    stats = jnp.where(lane == 5, jnp.sum(last[4:8], axis=1, keepdims=True) * (1.0 / groups), stats)
    for s in range(n_tiles):
        out_ref[s, 4:8, :] = stats


def finish_kernel(back_ref, hot_ref, dest_ref, modes_ref, eigen_ref, rows_ref, split_ref):
    n_tiles = back_ref.shape[0]
    obs = dest_ref.shape[1]
    count = n_tiles * obs
    total = back_ref[0]
    for t in range(1, n_tiles):
        total = total + back_ref[t]

    def stat(k, lane):
        return total[4 + k : 5 + k, lane : lane + 1]

    def g(k, j):
        return stat(k, k - j) * (1.0 / count)

    low = {}
    for j in range(MODES):
        d = g(j, j)
        for p in range(j):
            d = d - low[j, p] * low[j, p]
        low[j, j] = jnp.sqrt(d)
        for k in range(j + 1, MODES):
            v = g(k, j)
            for p in range(j):
                v = v - low[k, p] * low[j, p]
            low[k, j] = v / low[j, j]
    rows = n_tiles * MODES
    for t in range(n_tiles):
        rows_ref[t * MODES : (t + 1) * MODES, :] = back_ref[t, 0:MODES, :]
    a = rows_ref[...]
    hi = a.astype(BF16)
    rest = a - hi.astype(F32)
    mid = rest.astype(BF16)
    split_ref[0:rows, :] = hi
    split_ref[rows : 2 * rows, :] = mid
    split_ref[2 * rows : 3 * rows, :] = (rest - mid.astype(F32)).astype(BF16)
    chunk = 1024
    second = iota((8, chunk), 0) >> 2

    def finish(c, carry):
        at = pl.ds(pl.multiple_of(c * chunk, chunk), chunk)
        r = matmul(split_ref[...], hot_ref[:, at], NN)
        r = (r[0:rows] + r[rows : 2 * rows]) + r[2 * rows : 3 * rows]
        dest = jnp.broadcast_to(dest_ref[:, at], (8, chunk)) - second
        image = jnp.zeros((8, chunk), F32)
        for t in range(0, n_tiles, 2):
            image = image + jnp.where(dest == t, r[t * MODES : t * MODES + 8], 0.0)
        image = image[0:MODES] + image[MODES:8]
        done = []
        for k in range(MODES):
            v = image[k : k + 1]
            for p in range(k):
                v = v - low[k, p] * done[p]
            done.append(v / low[k, k])
            modes_ref[k : k + 1, at] = done[k]
        return carry

    lax.fori_loop(0, obs // chunk, finish, 0)
    eigen = jnp.zeros((1, 128), F32)
    for k in range(MODES):
        eigen = jnp.where(iota((1, 128), 1) == k, stat(k, 4) / stat(k, 5), eigen)
    eigen_ref[...] = eigen[0, 0:MODES]


VM = pl.BlockSpec(memory_space=pltpu.VMEM)
SM = pl.BlockSpec(memory_space=pltpu.SMEM)
ANY = pl.BlockSpec(memory_space=pl.ANY)
HBM = pl.BlockSpec(memory_space=pltpu.HBM)


def struct(shape, dtype):
    return jax.ShapeDtypeStruct(shape, dtype)


def on_device(members, weights, modes_in, obs_tile, obs_block):
    n_tiles = lax.axis_size("tile")
    n_groups = lax.axis_size("mem")
    obs, width = weights.shape
    count, levels, rows, ny = members.shape
    half = lax.axis_index("mem") % 2
    dest = obs_tile.reshape(1, obs)
    block = obs_block.reshape(1, obs)

    with jax.named_scope("swap"):
        give = lax.dynamic_slice_in_dim(members, 2 - 2 * half, 2, axis=1)
        got = lax.ppermute(give, "mem", [(m, m ^ 1) for m in range(n_groups)])
    with jax.named_scope("pack"):
        sent, hot, keep = pl.pallas_call(
            pack_kernel,
            in_specs=[SM] + [HBM] * 5,
            out_specs=[VM] * 3,
            out_shape=[
                struct((n_tiles, ROWS, 128), BF16),
                struct((128, obs), BF16),
                struct((count, 2, rows, ny), BF16),
            ],
            scratch_shapes=[
                pltpu.VMEM((obs, width), BF16),
                pltpu.VMEM((MODES, obs), F32),
                pltpu.VMEM((1, obs), jnp.int32),
                pltpu.VMEM((1, obs), jnp.int32),
                pltpu.VMEM((ROWS, obs), BF16),
                pltpu.VMEM((16, obs), F32),
                pltpu.VMEM((8 * ROWS, obs), BF16),
                pltpu.VMEM((8 * ROWS, obs), BF16),
                pltpu.SemaphoreType.DMA((5,)),
            ],
            compiler_params=vmem(60),
        )(half.reshape(1), weights, modes_in, dest, block, members)
    with jax.named_scope("forward"):
        recv = lax.all_to_all(sent, "tile", 0, 0, tiled=True)
    up = [(t, (t + 1) % n_tiles) for t in range(n_tiles)]
    down = [(b, a) for a, b in up]

    with jax.named_scope("member_edges"):
        def edge(first):
            both = jnp.concatenate([keep[:, :, first : first + HALO], got[:, :, first : first + HALO]], axis=0)
            return both.transpose(1, 0, 2, 3).reshape(2, 2 * count * HALO, ny)

        first, last = edge(0), edge(rows - HALO)
        m_low = lax.ppermute(last, "tile", up)
        m_high = lax.ppermute(first, "tile", down)
    scale = 1.0 / (TOTAL * (count * n_groups - 1))
    with jax.named_scope("pairs"):
        pairs, ends = pl.pallas_call(
            functools.partial(pair_kernel, scale),
            in_specs=[VM, VM],
            out_specs=[VM, VM],
            out_shape=[
                struct((len(POINTS), BY, rows, 128), F32),
                struct((2 * count, BY // 2, 16, 128), BF16),
            ],
            scratch_shapes=[
                pltpu.VMEM((2 * count, BY, rows + 16, 128), F32),
                pltpu.VMEM((2 * count, BY + 2 * HALO, rows, 128), F32),
                pltpu.VMEM((2 * count * 2 * rows, ny), F32),
            ],
            compiler_params=vmem(10),
            cost_estimate=cost(8),
        )(keep, got)

    with jax.named_scope("spread"):
        field, f_low, f_high = pl.pallas_call(
            spread_kernel,
            in_specs=[VM, ANY],
            out_specs=[VM] * 3,
            out_shape=[
                struct((MODES * BY, rows, 128), F32),
                struct((128, 128), F32),
                struct((128, 128), F32),
            ],
            scratch_shapes=[
                pltpu.VMEM((256, 8 * 128), BF16),
                pltpu.VMEM((256, 8 * 128), BF16),
            ],
            compiler_params=vmem(),
        )(recv, pairs)
    with jax.named_scope("spread_edges"):
        s_low = lax.ppermute(f_high, "tile", up)
        s_high = lax.ppermute(f_low, "tile", down)
    with jax.named_scope("pair_edges"):
        pairs_edge = pl.pallas_call(
            functools.partial(pair_edge_kernel, scale),
            in_specs=[VM, VM, VM, ANY],
            out_specs=VM,
            out_shape=struct((len(EDGE_POINTS), BY, 8, 128), F32),
            scratch_shapes=[
                pltpu.VMEM((2 * count, BY, 8 + 2 * HALO, 128), F32),
                pltpu.VMEM((2 * count, BY + 2 * HALO, 8, 128), F32),
                pltpu.VMEM((4 * 2 * count * HALO, ny), F32),
            ],
            compiler_params=vmem(6),
            cost_estimate=cost(3),
        )(ends, m_low, m_high, f_low)
    with jax.named_scope("images"):
        parts = pl.pallas_call(
            image_kernel,
            in_specs=[VM] * 6,
            out_specs=VM,
            out_shape=struct((n_tiles // 2 + 1, 8, 128), F32),
            scratch_shapes=[
                pltpu.VMEM((MODES, BY + 2 * HALO, rows, 128), F32),
                pltpu.VMEM((MODES, BY + 2 * HALO, 8, 128), F32),
                pltpu.VMEM((MODES, 2, 2 * HALO + 1, rows + 16, 128), F32),
                pltpu.VMEM((4, 128, 128), F32),
            ],
            compiler_params=vmem(),
        )(recv, field, s_low, s_high, pairs, pairs_edge)
    with jax.named_scope("group_sum"):
        for step in (1, 3):
            parts = parts + lax.ppermute(parts, "mem", [(m, m ^ step) for m in range(n_groups)])
        other = lax.ppermute(parts, "mem", [(m, n_groups - 1 - m) for m in range(n_groups)])
    with jax.named_scope("gram"):
        back = pl.pallas_call(
            functools.partial(gram_kernel, n_groups),
            in_specs=[VM, VM],
            out_specs=VM,
            out_shape=struct((n_tiles, 8, 128), F32),
            compiler_params=vmem(4),
        )(parts, other)
    with jax.named_scope("return"):
        back = lax.all_to_all(back, "tile", 0, 0, tiled=True)
    with jax.named_scope("finish"):
        modes_out, eigen = pl.pallas_call(
            finish_kernel,
            in_specs=[VM] * 3,
            out_specs=[VM] * 2,
            out_shape=[struct((MODES, obs), F32), struct((MODES,), F32)],
            scratch_shapes=[
                pltpu.VMEM((n_tiles * MODES, 128), F32),
                pltpu.VMEM((3 * n_tiles * MODES, 128), BF16),
            ],
            compiler_params=vmem(),
        )(back, hot, dest)
    return modes_out, eigen


def solution(mesh):
    in_specs = (
        P("mem", None, "tile", None),
        P("tile", None),
        P(None, "tile"),
        P("tile", None),
        P("tile"),
    )
    out_specs = (P(None, "tile"), P())
    return jax.shard_map(
        on_device, mesh=mesh, in_specs=in_specs, out_specs=out_specs, check_vma=False
    )
```

```python
import functools

import jax
import jax.numpy as jnp
from jax import lax
from jax.experimental import pallas as pl
from jax.experimental.pallas import tpu as pltpu
from jax.sharding import PartitionSpec as P

BX = 4
BY = 8
STEPS = 4
MODES = 4
ROWS = 80
TAIL = 64
HALO = 4
F32 = jnp.float32
BF16 = jnp.bfloat16


def stencil_points():
    counts = {(0, 0): 1}
    for _ in range(STEPS):
        wider = {}
        for (dx, dy), n in counts.items():
            for sx, sy in ((0, 0), (1, 0), (-1, 0), (0, 1), (0, -1)):
                key = (dx + sx, dy + sy)
                wider[key] = wider.get(key, 0) + n
        counts = wider
    return sorted((dx, dy, n) for (dx, dy), n in counts.items())


POINTS = [(dx, dy, n, i) for i, (dx, dy, n) in enumerate(stencil_points())]
EDGE_POINTS = [p for p in POINTS if p[0] > 0]
EDGE_POINTS = [(dx, dy, n, i) for i, (dx, dy, n, _) in enumerate(EDGE_POINTS)]
TOTAL = float(5**STEPS)

PAIRS_KIB = 65536 - 12000

NT = (((1,), (1,)), ((), ()))
NN = (((1,), (0,)), ((), ()))


def matmul(a, b, dims):
    return lax.dot_general(a, b, dims, preferred_element_type=F32)


def iota(shape, dim):
    return lax.broadcasted_iota(jnp.int32, shape, dim)


def cost(us):
    return pl.CostEstimate(flops=0, bytes_accessed=us * 3_690_000, transcendentals=0)


def vmem(limit=16):
    return pltpu.CompilerParams(vmem_limit_bytes=limit << 20)


def pack_kernel(
    half_ref, w_any, modes_any, dest_any, block_any, members_any, out_ref, hot_ref, keep_ref,
    w_ref, modes_ref, dest_ref, block_ref, x_ref, tail_ref, xa_ref, xb_ref, sems,
):
    n_tiles = out_ref.shape[0]
    obs = w_ref.shape[0]
    half = half_ref[0]
    pairs = (
        (dest_any, dest_ref),
        (w_any, w_ref),
        (modes_any, modes_ref),
        (block_any, block_ref),
        (members_any.at[:, pl.ds(2 * half, 2)], keep_ref),
    )
    copies = [pltpu.make_async_copy(a, b, sems.at[i]) for i, (a, b) in enumerate(pairs)]
    for copy in copies:
        copy.start()
    copies[0].wait()
    chunk = 256
    upper = jnp.where(iota((chunk, chunk), 0) < iota((chunk, chunk), 1), 1.0, 0.0).astype(BF16)
    off = jnp.zeros((n_tiles, 1), F32)
    for c in range(obs // chunk):
        at = slice(c * chunk, (c + 1) * chunk)
        d = jnp.where(iota((n_tiles, chunk), 0) == dest_ref[:, at], 1.0, 0.0)
        before = matmul(d.astype(BF16), upper, NN) + off
        rank = jnp.sum(d * before, axis=0, keepdims=True).astype(jnp.int32)
        hot_ref[:, at] = jnp.where(iota((128, chunk), 0) == rank, 1.0, 0.0).astype(BF16)
        off = off + jnp.sum(d, axis=1, keepdims=True)
    for copy in copies[1:]:
        copy.wait()
    q = iota((TAIL, 128), 0)
    source = (2 * half + (q >> 5)) * 32 + (q & 3) * 8 + ((q >> 2) & 7)
    order = jnp.where(iota((TAIL, 128), 1) == source, 1.0, 0.0).astype(BF16)
    x_ref[0:TAIL, :] = matmul(order, w_ref[...], NT).astype(BF16)
    m = modes_ref[...]
    hi = m.astype(BF16).astype(F32)
    mid = (m - hi).astype(BF16).astype(F32)
    lo = (m - hi) - mid
    tail_ref[0:4, :] = hi
    tail_ref[4:8, :] = mid
    tail_ref[8:12, :] = lo
    tail_ref[12:13, :] = (block_ref[...] + 1).astype(F32)
    tail_ref[13:16, :] = jnp.zeros((3, obs), F32)
    x_ref[TAIL:ROWS, :] = tail_ref[...].astype(BF16)
    group = 8
    rows = group * ROWS

    def send(g, carry):
        for part, xm_ref in enumerate((xa_ref, xb_ref)):
            first = (2 * g + part) * group
            for t in range(group):
                here = jnp.where(dest_ref[...] == first + t, 1.0, 0.0)
                here = jnp.broadcast_to(here, (16, obs)).astype(BF16)
                for r in range(ROWS // 16):
                    row = t * ROWS + r * 16
                    xm_ref[row : row + 16, :] = x_ref[r * 16 : r * 16 + 16, :] * here
            sent = matmul(xm_ref[...], hot_ref[...], NT)
            out_ref[pl.ds(first, group)] = sent.astype(BF16).reshape(group, ROWS, 128)
        return carry

    lax.fori_loop(0, n_tiles // (2 * group), send, 0)


def extend(ext_ref, lead):
    lane = iota((ext_ref.shape[-2], 128), 1) & 63
    for n in range(HALO):
        low = pltpu.roll(ext_ref[lead, HALO + BY - HALO + n], 1, 1)
        ext_ref[lead, n] = jnp.where(lane == 0, ext_ref[lead, HALO + HALO - 1 - n], low)
        high = pltpu.roll(ext_ref[lead, HALO + n], 127, 1)
        ext_ref[lead, HALO + BY + n] = jnp.where(lane == 63, ext_ref[lead, HALO + BY - 1 - n], high)


def spread_rows(x, move):
    return matmul(x, move, NN)


def mover(ny):
    lane = iota((ny, ny), 1)
    return jnp.where(iota((ny, ny), 0) == (lane & 63) * BY + (lane >> 6), 1.0, 0.0).astype(BF16)


def join(first, second, p):
    a = first[:, p * 128 : (p + 1) * 128]
    b = second[:, p * 128 : (p + 1) * 128]
    left = iota(a.shape, 1) < 64
    return jnp.where(left, a, pltpu.roll(b, 64, 1)), jnp.where(left, pltpu.roll(a, 64, 1), b)


def pair_sums(center_of, ext_ref, out_ref, scale, c, at, points):
    total = ext_ref.shape[0]

    def member(m, sums):
        ext = {dy: ext_ref[m, HALO + c + dy, at : at + 8, :] for _, dy, _, _ in points}
        center = {dx: center_of(m, dx) for dx, _, _, _ in points}
        return tuple(s + center[dx] * ext[dy] for s, (dx, dy, _, _) in zip(sums, points))

    sums = lax.fori_loop(
        0, total, member, tuple(jnp.zeros((8, 128), F32) for _ in points), unroll=4
    )
    for s, (dx, dy, n, i) in zip(sums, points):
        out_ref[i, c, at : at + 8, :] = s * (n * scale)


def pair_kernel(
    scale, keep_ref, got_ref, out_any, ends_ref, out_ref, center_ref, ext_ref, y_ref, sem
):
    count = got_ref.shape[0]
    total = 2 * count
    rows = got_ref.shape[2]
    ny = got_ref.shape[3]
    move = mover(ny)
    side = count * 2 * rows
    for i, ref in enumerate((keep_ref, got_ref)):
        y_ref[i * side : (i + 1) * side, :] = spread_rows(ref[...].reshape(side, ny), move)

    def place(m, carry):
        row = pl.multiple_of(m * 2 * rows, 2 * rows)
        first = y_ref[pl.ds(row, rows), :]
        second = y_ref[pl.ds(row + rows, rows), :]
        zero = jnp.zeros((8, 128), F32)
        for p in range(BY // 2):
            both = join(first, second, p)
            ends = [both[0][rows - HALO :], both[0][0:HALO], both[1][rows - HALO :], both[1][0:HALO]]
            ends_ref[m, p] = jnp.concatenate(ends, axis=0).astype(BF16)
            for i, v in enumerate(both):
                c = 2 * p + i
                ext_ref[m, HALO + c] = v
                center_ref[m, c, 0:8, :] = zero
                center_ref[m, c, 8 : 8 + rows, :] = v
                center_ref[m, c, 8 + rows : 16 + rows, :] = zero
        extend(ext_ref, m)
        return carry

    lax.fori_loop(0, total, place, 0, unroll=4)

    def plane(c, carry):
        for v in range(rows // 8):

            def center_of(m, dx):
                return center_ref[m, c, 8 + v * 8 - dx : 16 + v * 8 - dx, :]

            pair_sums(center_of, ext_ref, out_ref, scale, c, v * 8, POINTS)
        pltpu.make_async_copy(out_ref.at[:, c], out_any.at[:, c], sem).start()
        return carry

    lax.fori_loop(0, BY, plane, 0)
    pltpu.make_async_copy(out_ref, out_any, sem).wait()


def pair_edge_kernel(scale, ends_ref, low_ref, high_ref, after_ref, out_ref, center_ref, ext_ref, y_ref):
    total = center_ref.shape[0]
    ny = low_ref.shape[3]
    side = 2 * total * HALO
    move = mover(ny)
    for start, ref in ((0, high_ref), (side, low_ref)):
        rows = [ref[m, l].astype(F32) for l in range(2) for m in range(total)]
        y_ref[start : start + side, :] = spread_rows(jnp.concatenate(rows, axis=0).astype(BF16), move)

    def place(m, carry):
        blocks = []
        for start in (0, side):
            row = pl.multiple_of(start + m * 2 * HALO, 8)
            blocks.append((y_ref[pl.ds(row, 8), :], y_ref[pl.ds(row + side // 2, 8), :]))
        top = iota((8, 128), 0) < HALO
        for p in range(BY // 2):
            for i, (high, low) in enumerate(zip(join(*blocks[0], p), join(*blocks[1], p))):
                ext_ref[2 * m, HALO + 2 * p + i] = jnp.where(top, high, pltpu.roll(low, HALO, 0))
                ext_ref[2 * m + 1, HALO + 2 * p + i] = jnp.where(top, pltpu.roll(high, HALO, 0), low)
        extend(ext_ref, 2 * m)
        extend(ext_ref, 2 * m + 1)
        for n in range(2):
            for p in range(BY // 2):
                ends = ends_ref[2 * m + n, p].astype(F32)
                for i in range(2):
                    center_ref[2 * m + n, 2 * p + i, 0:HALO, :] = ends[8 * i : 8 * i + HALO]
                    center_ref[2 * m + n, 2 * p + i, HALO : HALO + 8, :] = jnp.zeros((8, 128), F32)
                    center_ref[2 * m + n, 2 * p + i, HALO + 8 :, :] = ends[8 * i + HALO : 8 * i + 8]
        return carry

    lax.fori_loop(0, total // 2, place, 0, unroll=2)

    def plane(c, carry):
        def center_of(m, dx):
            return center_ref[m, c, HALO - dx : HALO + 8 - dx, :] + center_ref[m, c, HALO + dx : HALO + 8 + dx, :]

        pair_sums(center_of, ext_ref, out_ref, scale, c, 0, EDGE_POINTS)
        return carry

    lax.fori_loop(0, BY, plane, 0)


def block_hot(tail):
    return jnp.where((iota((256, 128), 0) + 1).astype(F32) == tail[12:13, :], 1.0, 0.0).astype(BF16)


def spread_kernel(recv_ref, after_ref, out_ref, low_ref, high_ref, g_ref, h_ref):
    n_tiles = recv_ref.shape[0]

    group = 8

    def sources(g, total):
        for j in range(group):
            at = slice(j * 128, (j + 1) * 128)
            w = recv_ref[g * group + j, 0:TAIL, :].astype(F32)
            tail = recv_ref[g * group + j, TAIL:ROWS, :].astype(F32)
            h_ref[:, at] = block_hot(tail)
            for l in range(2):
                for k in range(MODES):
                    row = l * 128 + k * 32
                    g_ref[row : row + 32, at] = (w[l * 32 : l * 32 + 32, :] * tail[k : k + 1, :]).astype(BF16)
        return total + matmul(g_ref[...], h_ref[...], NT)

    r = lax.fori_loop(0, n_tiles // group, sources, jnp.zeros((256, 256), F32))
    for i in range(4):
        t = jnp.concatenate([r[0:128, i * 64 : i * 64 + 64], r[128:256, i * 64 : i * 64 + 64]], axis=1)
        if i == 0:
            low_ref[...] = t
        if i == 3:
            high_ref[...] = t
        for n in range(MODES * BY):
            out_ref[n, i * 4 : i * 4 + 4, :] = t[n * 4 : n * 4 + 4, :]


def image_kernel(recv_ref, f_ref, low_ref, high_ref, c_ref, ce_ref, out_ref, ext_ref, side_ref, q_ref, t_ref):
    n_tiles = recv_ref.shape[0]
    rows = f_ref.shape[1]
    for k in range(MODES):
        for c in range(BY):
            n = k * BY + c
            ext_ref[k, HALO + c] = f_ref[n]
            side_ref[k, HALO + c, 0:HALO, :] = high_ref[n * 4 : n * 4 + 4, :]
            side_ref[k, HALO + c, HALO:8, :] = low_ref[n * 4 : n * 4 + 4, :]
        extend(ext_ref, k)
        extend(side_ref, k)

    def weigh(ref, v, c, points, weights):
        sums = [{} for _ in range(MODES)]
        for dx, dy, n, i in points:
            weight = weights[i, c, v * 8 : v * 8 + 8, :]
            for k in range(MODES):
                term = weight * ref[k, HALO + c + dy, v * 8 : v * 8 + 8, :]
                sums[k][dx] = sums[k][dx] + term if dx in sums[k] else term
        return sums

    def plane(cp, carry):
        for j in range(2):
            c = 2 * cp + j
            for v in range(rows // 8):
                for k, sums in enumerate(weigh(ext_ref, v, c, POINTS, c_ref)):
                    for dx, q in sums.items():
                        q_ref[k, j, dx + HALO, 8 + v * 8 : 16 + v * 8, :] = q
            for k, sums in enumerate(weigh(side_ref, 0, c, EDGE_POINTS, ce_ref)):
                for dx, q in sums.items():
                    q_ref[k, j, HALO - dx, 0:8, :] = q
                    q_ref[k, j, HALO + dx, rows + 8 : rows + 16, :] = q
        for k in range(MODES):
            for i in range(4):
                both = []
                for j in range(2):
                    at = 8 + i * 4
                    v = q_ref[k, j, HALO, at : at + 4, :]
                    for dx in range(-HALO, HALO + 1):
                        if dx != 0:
                            v = v + q_ref[k, j, dx + HALO, at + dx : at + dx + 4, :]
                    both.append(v)
                row = pl.multiple_of(k * 32 + cp * 8, 8)
                t_ref[i, pl.ds(row, 8), :] = jnp.concatenate(both, axis=0)
        return carry

    lax.fori_loop(0, BY // 2, plane, 0)
    cov = jnp.concatenate(
        [
            jnp.concatenate([t_ref[i, :, l * 64 : l * 64 + 64] for i in range(4)], axis=1)
            for l in range(2)
        ],
        axis=0,
    )
    hi = cov.astype(BF16)
    lo = (cov - hi.astype(F32)).astype(BF16)
    both = jnp.concatenate([hi, lo], axis=0)
    group = 8

    def image(g, carry):
        cross, square = carry
        hots = [block_hot(recv_ref[g * group + j, TAIL:ROWS, :].astype(F32)) for j in range(group)]
        picked = matmul(both, jnp.concatenate(hots, axis=1), NN)
        picked = picked[0:256] + picked[256:512]
        for j in range(group):
            s = g * group + j
            w = recv_ref[s, 0:TAIL, :].astype(F32)
            tail = recv_ref[s, TAIL:ROWS, :].astype(F32)
            first = (j % 2) * 4
            pair = g * (group // 2) + j // 2
            for k in range(MODES):
                part = picked[k * 32 : k * 32 + 32, j * 128 : (j + 1) * 128] * w[0:32]
                part = part + picked[128 + k * 32 : 160 + k * 32, j * 128 : (j + 1) * 128] * w[32:64]
                out_ref[pair, first + k : first + k + 1, :] = jnp.sum(part, axis=0, keepdims=True)
            mode = tail[0:4] + tail[4:8] + tail[8:12]
            cross = cross + mode * out_ref[pair, first : first + 4, :]
            square = square + mode * mode
        return cross, square

    zero = jnp.zeros((MODES, 128), F32)
    cross, square = lax.fori_loop(0, n_tiles // group, image, (zero, zero))
    out_ref[n_tiles // 2, 0:4, :] = cross
    out_ref[n_tiles // 2, 4:8, :] = square


def gram_kernel(groups, parts_ref, other_ref, out_ref):
    n_tiles = out_ref.shape[0]
    pairs = n_tiles // 2
    sums = [jnp.zeros((8, 128), F32) for _ in range(MODES)]
    lane = iota((4, 128), 1)
    for p in range(pairs):
        z = parts_ref[p] + other_ref[p]
        out_ref[2 * p, 0:4, :] = z[0:4]
        out_ref[2 * p + 1, 0:4, :] = z[4:8]
        for d in range(MODES):
            sums[d] = sums[d] + z * (z if d == 0 else pltpu.roll(z, d, 0))
    last = parts_ref[pairs] + other_ref[pairs]
    stats = jnp.zeros((4, 128), F32)
    for d in range(MODES):
        both = sums[d][0:4] + sums[d][4:8]
        stats = jnp.where(lane == d, jnp.sum(both, axis=1, keepdims=True), stats)
    stats = jnp.where(lane == 4, jnp.sum(last[0:4], axis=1, keepdims=True), stats)
    stats = jnp.where(lane == 5, jnp.sum(last[4:8], axis=1, keepdims=True) * (1.0 / groups), stats)
    for s in range(n_tiles):
        out_ref[s, 4:8, :] = stats


def finish_kernel(back_ref, hot_ref, dest_ref, modes_ref, eigen_ref, rows_ref, split_ref):
    n_tiles = back_ref.shape[0]
    obs = dest_ref.shape[1]
    count = n_tiles * obs
    total = back_ref[0]
    for t in range(1, n_tiles):
        total = total + back_ref[t]

    def stat(k, lane):
        return total[4 + k : 5 + k, lane : lane + 1]

    def g(k, j):
        return stat(k, k - j) * (1.0 / count)

    low = {}
    for j in range(MODES):
        d = g(j, j)
        for p in range(j):
            d = d - low[j, p] * low[j, p]
        low[j, j] = jnp.sqrt(d)
        for k in range(j + 1, MODES):
            v = g(k, j)
            for p in range(j):
                v = v - low[k, p] * low[j, p]
            low[k, j] = v / low[j, j]
    rows = n_tiles * MODES
    for t in range(n_tiles):
        rows_ref[t * MODES : (t + 1) * MODES, :] = back_ref[t, 0:MODES, :]
    a = rows_ref[...]
    hi = a.astype(BF16)
    rest = a - hi.astype(F32)
    mid = rest.astype(BF16)
    split_ref[0:rows, :] = hi
    split_ref[rows : 2 * rows, :] = mid
    split_ref[2 * rows : 3 * rows, :] = (rest - mid.astype(F32)).astype(BF16)
    chunk = 1024
    second = iota((8, chunk), 0) >> 2

    def finish(c, carry):
        at = pl.ds(pl.multiple_of(c * chunk, chunk), chunk)
        r = matmul(split_ref[...], hot_ref[:, at], NN)
        r = (r[0:rows] + r[rows : 2 * rows]) + r[2 * rows : 3 * rows]
        dest = jnp.broadcast_to(dest_ref[:, at], (8, chunk)) - second
        image = jnp.zeros((8, chunk), F32)
        for t in range(0, n_tiles, 2):
            image = image + jnp.where(dest == t, r[t * MODES : t * MODES + 8], 0.0)
        image = image[0:MODES] + image[MODES:8]
        done = []
        for k in range(MODES):
            v = image[k : k + 1]
            for p in range(k):
                v = v - low[k, p] * done[p]
            done.append(v / low[k, k])
            modes_ref[k : k + 1, at] = done[k]
        return carry

    lax.fori_loop(0, obs // chunk, finish, 0, unroll=True)
    eigen = jnp.zeros((1, 128), F32)
    for k in range(MODES):
        eigen = jnp.where(iota((1, 128), 1) == k, stat(k, 4) / stat(k, 5), eigen)
    eigen_ref[...] = eigen[0, 0:MODES]


VM = pl.BlockSpec(memory_space=pltpu.VMEM)
SM = pl.BlockSpec(memory_space=pltpu.SMEM)
ANY = pl.BlockSpec(memory_space=pl.ANY)
HBM = pl.BlockSpec(memory_space=pltpu.HBM)


def struct(shape, dtype):
    return jax.ShapeDtypeStruct(shape, dtype)


def on_device(members, weights, modes_in, obs_tile, obs_block):
    n_tiles = lax.axis_size("tile")
    n_groups = lax.axis_size("mem")
    obs, width = weights.shape
    count, levels, rows, ny = members.shape
    half = lax.axis_index("mem") % 2
    dest = obs_tile.reshape(1, obs)
    block = obs_block.reshape(1, obs)

    with jax.named_scope("swap"):
        give = lax.dynamic_slice_in_dim(members, 2 - 2 * half, 2, axis=1)
        got = lax.ppermute(give, "mem", [(m, m ^ 1) for m in range(n_groups)])
    with jax.named_scope("pack"):
        sent, hot, keep = pl.pallas_call(
            pack_kernel,
            in_specs=[SM] + [HBM] * 5,
            out_specs=[VM] * 3,
            out_shape=[
                struct((n_tiles, ROWS, 128), BF16),
                struct((128, obs), BF16),
                struct((count, 2, rows, ny), BF16),
            ],
            scratch_shapes=[
                pltpu.VMEM((obs, width), BF16),
                pltpu.VMEM((MODES, obs), F32),
                pltpu.VMEM((1, obs), jnp.int32),
                pltpu.VMEM((1, obs), jnp.int32),
                pltpu.VMEM((ROWS, obs), BF16),
                pltpu.VMEM((16, obs), F32),
                pltpu.VMEM((8 * ROWS, obs), BF16),
                pltpu.VMEM((8 * ROWS, obs), BF16),
                pltpu.SemaphoreType.DMA((5,)),
            ],
            compiler_params=vmem(60),
        )(half.reshape(1), weights, modes_in, dest, block, members)
    with jax.named_scope("forward"):
        recv = lax.all_to_all(sent, "tile", 0, 0, tiled=True)
    up = [(t, (t + 1) % n_tiles) for t in range(n_tiles)]
    down = [(b, a) for a, b in up]

    with jax.named_scope("member_edges"):
        def edge(first):
            return jnp.concatenate([keep[:, :, first : first + HALO], got[:, :, first : first + HALO]], axis=0)

        first, last = edge(0), edge(rows - HALO)
        m_low = lax.ppermute(last, "tile", up)
        m_high = lax.ppermute(first, "tile", down)
    scale = 1.0 / (TOTAL * (count * n_groups - 1))
    with jax.named_scope("pairs"):
        pairs, ends = pl.pallas_call(
            functools.partial(pair_kernel, scale),
            in_specs=[VM, VM],
            out_specs=[HBM, VM],
            out_shape=[
                struct((len(POINTS), BY, rows, 128), F32),
                struct((2 * count, BY // 2, 16, 128), BF16),
            ],
            scratch_shapes=[
                pltpu.VMEM((len(POINTS), BY, rows, 128), F32),
                pltpu.VMEM((2 * count, BY, rows + 16, 128), F32),
                pltpu.VMEM((2 * count, BY + 2 * HALO, rows, 128), F32),
                pltpu.VMEM((2 * count * 2 * rows, ny), F32),
                pltpu.SemaphoreType.DMA,
            ],
            compiler_params=pltpu.CompilerParams(vmem_limit_bytes=PAIRS_KIB << 10),
            cost_estimate=cost(8),
        )(keep, got)

    with jax.named_scope("spread"):
        field, f_low, f_high = pl.pallas_call(
            spread_kernel,
            in_specs=[VM, ANY],
            out_specs=[VM] * 3,
            out_shape=[
                struct((MODES * BY, rows, 128), F32),
                struct((128, 128), F32),
                struct((128, 128), F32),
            ],
            scratch_shapes=[
                pltpu.VMEM((256, 8 * 128), BF16),
                pltpu.VMEM((256, 8 * 128), BF16),
            ],
            compiler_params=vmem(),
        )(recv, ends)
    with jax.named_scope("spread_edges"):
        s_low = lax.ppermute(f_high, "tile", up)
        s_high = lax.ppermute(f_low, "tile", down)
    with jax.named_scope("pair_edges"):
        pairs_edge = pl.pallas_call(
            functools.partial(pair_edge_kernel, scale),
            in_specs=[VM, VM, VM, ANY],
            out_specs=VM,
            out_shape=struct((len(EDGE_POINTS), BY, 8, 128), F32),
            scratch_shapes=[
                pltpu.VMEM((2 * count, BY, 8 + 2 * HALO, 128), F32),
                pltpu.VMEM((2 * count, BY + 2 * HALO, 8, 128), F32),
                pltpu.VMEM((4 * 2 * count * HALO, ny), F32),
            ],
            compiler_params=vmem(6),
            cost_estimate=cost(3),
        )(ends, m_low, m_high, f_low)
    with jax.named_scope("images"):
        parts = pl.pallas_call(
            image_kernel,
            in_specs=[VM] * 6,
            out_specs=VM,
            out_shape=struct((n_tiles // 2 + 1, 8, 128), F32),
            scratch_shapes=[
                pltpu.VMEM((MODES, BY + 2 * HALO, rows, 128), F32),
                pltpu.VMEM((MODES, BY + 2 * HALO, 8, 128), F32),
                pltpu.VMEM((MODES, 2, 2 * HALO + 1, rows + 16, 128), F32),
                pltpu.VMEM((4, 128, 128), F32),
            ],
            compiler_params=vmem(),
        )(recv, field, s_low, s_high, pairs, pairs_edge)
    with jax.named_scope("group_sum"):
        for step in (1, 3):
            parts = parts + lax.ppermute(parts, "mem", [(m, m ^ step) for m in range(n_groups)])
        other = lax.ppermute(parts, "mem", [(m, n_groups - 1 - m) for m in range(n_groups)])
    with jax.named_scope("gram"):
        back = pl.pallas_call(
            functools.partial(gram_kernel, n_groups),
            in_specs=[VM, VM],
            out_specs=VM,
            out_shape=struct((n_tiles, 8, 128), F32),
            compiler_params=vmem(4),
        )(parts, other)
    with jax.named_scope("return"):
        back = lax.all_to_all(back, "tile", 0, 0, tiled=True)
    with jax.named_scope("finish"):
        modes_out, eigen = pl.pallas_call(
            finish_kernel,
            in_specs=[VM] * 3,
            out_specs=[VM] * 2,
            out_shape=[struct((MODES, obs), F32), struct((MODES,), F32)],
            scratch_shapes=[
                pltpu.VMEM((n_tiles * MODES, 128), F32),
                pltpu.VMEM((3 * n_tiles * MODES, 128), BF16),
            ],
            compiler_params=vmem(),
        )(back, hot, dest)
    return modes_out, eigen


def solution(mesh):
    in_specs = (
        P("mem", None, "tile", None),
        P("tile", None),
        P(None, "tile"),
        P("tile", None),
        P("tile"),
    )
    out_specs = (P(None, "tile"), P())
    return jax.shard_map(
        on_device, mesh=mesh, in_specs=in_specs, out_specs=out_specs, check_vma=False
    )
```

```python
import functools

import jax
import jax.numpy as jnp
from jax import lax
from jax.experimental import pallas as pl
from jax.experimental.pallas import tpu as pltpu
from jax.sharding import PartitionSpec as P

BX = 4
BY = 8
STEPS = 4
MODES = 4
ROWS = 80
TAIL = 64
HALO = 4
F32 = jnp.float32
BF16 = jnp.bfloat16


def stencil_points():
    counts = {(0, 0): 1}
    for _ in range(STEPS):
        wider = {}
        for (dx, dy), n in counts.items():
            for sx, sy in ((0, 0), (1, 0), (-1, 0), (0, 1), (0, -1)):
                key = (dx + sx, dy + sy)
                wider[key] = wider.get(key, 0) + n
        counts = wider
    return sorted((dx, dy, n) for (dx, dy), n in counts.items())


POINTS = [(dx, dy, n, i) for i, (dx, dy, n) in enumerate(stencil_points())]
EDGE_POINTS = [p for p in POINTS if p[0] > 0]
EDGE_POINTS = [(dx, dy, n, i) for i, (dx, dy, n, _) in enumerate(EDGE_POINTS)]
TOTAL = float(5**STEPS)
CUT = len([p for p in POINTS if p[0] <= 0])

PAIRS_KIB = 65536 - 12000

NT = (((1,), (1,)), ((), ()))
NN = (((1,), (0,)), ((), ()))


def matmul(a, b, dims):
    return lax.dot_general(a, b, dims, preferred_element_type=F32)


def iota(shape, dim):
    return lax.broadcasted_iota(jnp.int32, shape, dim)


def cost(us):
    return pl.CostEstimate(flops=0, bytes_accessed=us * 3_690_000, transcendentals=0)


def vmem(limit=16):
    return pltpu.CompilerParams(vmem_limit_bytes=limit << 20)


def pack_kernel(
    half_ref, w_any, modes_any, dest_any, block_any, members_any, out_ref, hot_ref, keep_ref,
    w_ref, modes_ref, dest_ref, block_ref, x_ref, tail_ref, xa_ref, xb_ref, sems,
):
    n_tiles = out_ref.shape[0]
    obs = w_ref.shape[0]
    half = half_ref[0]
    pairs = (
        (dest_any, dest_ref),
        (w_any, w_ref),
        (modes_any, modes_ref),
        (block_any, block_ref),
        (members_any.at[:, pl.ds(2 * half, 2)], keep_ref),
    )
    copies = [pltpu.make_async_copy(a, b, sems.at[i]) for i, (a, b) in enumerate(pairs)]
    for copy in copies:
        copy.start()
    copies[0].wait()
    chunk = 256
    upper = jnp.where(iota((chunk, chunk), 0) < iota((chunk, chunk), 1), 1.0, 0.0).astype(BF16)
    off = jnp.zeros((n_tiles, 1), F32)
    for c in range(obs // chunk):
        at = slice(c * chunk, (c + 1) * chunk)
        d = jnp.where(iota((n_tiles, chunk), 0) == dest_ref[:, at], 1.0, 0.0)
        before = matmul(d.astype(BF16), upper, NN) + off
        rank = jnp.sum(d * before, axis=0, keepdims=True).astype(jnp.int32)
        hot_ref[:, at] = jnp.where(iota((128, chunk), 0) == rank, 1.0, 0.0).astype(BF16)
        off = off + jnp.sum(d, axis=1, keepdims=True)
    for copy in copies[1:]:
        copy.wait()
    q = iota((TAIL, 128), 0)
    source = (2 * half + (q >> 5)) * 32 + (q & 3) * 8 + ((q >> 2) & 7)
    order = jnp.where(iota((TAIL, 128), 1) == source, 1.0, 0.0).astype(BF16)
    x_ref[0:TAIL, :] = matmul(order, w_ref[...], NT).astype(BF16)
    m = modes_ref[...]
    hi = m.astype(BF16).astype(F32)
    mid = (m - hi).astype(BF16).astype(F32)
    lo = (m - hi) - mid
    tail_ref[0:4, :] = hi
    tail_ref[4:8, :] = mid
    tail_ref[8:12, :] = lo
    tail_ref[12:13, :] = (block_ref[...] + 1).astype(F32)
    tail_ref[13:16, :] = jnp.zeros((3, obs), F32)
    x_ref[TAIL:ROWS, :] = tail_ref[...].astype(BF16)
    group = 8
    rows = group * ROWS

    def send(g, carry):
        for part, xm_ref in enumerate((xa_ref, xb_ref)):
            first = (2 * g + part) * group
            for t in range(group):
                here = jnp.where(dest_ref[...] == first + t, 1.0, 0.0)
                here = jnp.broadcast_to(here, (16, obs)).astype(BF16)
                for r in range(ROWS // 16):
                    row = t * ROWS + r * 16
                    xm_ref[row : row + 16, :] = x_ref[r * 16 : r * 16 + 16, :] * here
            sent = matmul(xm_ref[...], hot_ref[...], NT)
            out_ref[pl.ds(first, group)] = sent.astype(BF16).reshape(group, ROWS, 128)
        return carry

    lax.fori_loop(0, n_tiles // (2 * group), send, 0, unroll=True)


def extend(ext_ref, lead):
    lane = iota((ext_ref.shape[-2], 128), 1) & 63
    for n in range(HALO):
        low = pltpu.roll(ext_ref[lead, HALO + BY - HALO + n], 1, 1)
        ext_ref[lead, n] = jnp.where(lane == 0, ext_ref[lead, HALO + HALO - 1 - n], low)
        high = pltpu.roll(ext_ref[lead, HALO + n], 127, 1)
        ext_ref[lead, HALO + BY + n] = jnp.where(lane == 63, ext_ref[lead, HALO + BY - 1 - n], high)


def spread_rows(x, move):
    return matmul(x, move, NN)


def mover(ny):
    lane = iota((ny, ny), 1)
    return jnp.where(iota((ny, ny), 0) == (lane & 63) * BY + (lane >> 6), 1.0, 0.0).astype(BF16)


def join(first, second, p):
    a = first[:, p * 128 : (p + 1) * 128]
    b = second[:, p * 128 : (p + 1) * 128]
    left = iota(a.shape, 1) < 64
    return jnp.where(left, a, pltpu.roll(b, 64, 1)), jnp.where(left, pltpu.roll(a, 64, 1), b)


def pair_sums(center_of, ext_ref, out_ref, scale, c, at, points):
    total = ext_ref.shape[0]

    def member(m, sums):
        ext = {dy: ext_ref[m, HALO + c + dy, at : at + 8, :] for _, dy, _, _ in points}
        center = {dx: center_of(m, dx) for dx, _, _, _ in points}
        return tuple(s + center[dx] * ext[dy] for s, (dx, dy, _, _) in zip(sums, points))

    sums = lax.fori_loop(
        0, total, member, tuple(jnp.zeros((8, 128), F32) for _ in points), unroll=4
    )
    for s, (dx, dy, n, i) in zip(sums, points):
        out_ref[i, c, at : at + 8, :] = s * (n * scale)


def pair_kernel(
    scale, keep_ref, got_ref, behind_any, ahead_any, ends_ref, out_ref, center_ref, ext_ref, y_ref, sems
):
    count = got_ref.shape[0]
    total = 2 * count
    rows = got_ref.shape[2]
    ny = got_ref.shape[3]
    move = mover(ny)
    side = count * 2 * rows
    for i, ref in enumerate((keep_ref, got_ref)):
        y_ref[i * side : (i + 1) * side, :] = spread_rows(ref[...].reshape(side, ny), move)

    def place(m, carry):
        row = pl.multiple_of(m * 2 * rows, 2 * rows)
        first = y_ref[pl.ds(row, rows), :]
        second = y_ref[pl.ds(row + rows, rows), :]
        zero = jnp.zeros((8, 128), F32)
        for p in range(BY // 2):
            both = join(first, second, p)
            ends = [both[0][rows - HALO :], both[0][0:HALO], both[1][rows - HALO :], both[1][0:HALO]]
            ends_ref[m, p] = jnp.concatenate(ends, axis=0).astype(BF16)
            for i, v in enumerate(both):
                c = 2 * p + i
                ext_ref[m, HALO + c] = v
                center_ref[m, c, 0:8, :] = zero
                center_ref[m, c, 8 : 8 + rows, :] = v
                center_ref[m, c, 8 + rows : 16 + rows, :] = zero
        extend(ext_ref, m)
        return carry

    lax.fori_loop(0, total, place, 0, unroll=4)

    def plane(c, carry):
        for v in range(rows // 8):

            def center_of(m, dx):
                return center_ref[m, c, 8 + v * 8 - dx : 16 + v * 8 - dx, :]

            pair_sums(center_of, ext_ref, out_ref, scale, c, v * 8, POINTS)
        pltpu.make_async_copy(out_ref.at[0:CUT, c], behind_any.at[:, c], sems.at[0]).start()
        pltpu.make_async_copy(out_ref.at[CUT:, c], ahead_any.at[:, c], sems.at[1]).start()
        return carry

    lax.fori_loop(0, BY, plane, 0)
    pltpu.make_async_copy(out_ref.at[0:CUT], behind_any, sems.at[0]).wait()
    pltpu.make_async_copy(out_ref.at[CUT:], ahead_any, sems.at[1]).wait()


def pair_edge_kernel(scale, ends_ref, low_ref, high_ref, after_ref, out_ref, center_ref, ext_ref, y_ref):
    total = center_ref.shape[0]
    ny = low_ref.shape[3]
    side = 2 * total * HALO
    move = mover(ny)
    for start, ref in ((0, high_ref), (side, low_ref)):
        rows = [ref[m, l].astype(F32) for l in range(2) for m in range(total)]
        y_ref[start : start + side, :] = spread_rows(jnp.concatenate(rows, axis=0).astype(BF16), move)

    def place(m, carry):
        blocks = []
        for start in (0, side):
            row = pl.multiple_of(start + m * 2 * HALO, 8)
            blocks.append((y_ref[pl.ds(row, 8), :], y_ref[pl.ds(row + side // 2, 8), :]))
        top = iota((8, 128), 0) < HALO
        for p in range(BY // 2):
            for i, (high, low) in enumerate(zip(join(*blocks[0], p), join(*blocks[1], p))):
                ext_ref[2 * m, HALO + 2 * p + i] = jnp.where(top, high, pltpu.roll(low, HALO, 0))
                ext_ref[2 * m + 1, HALO + 2 * p + i] = jnp.where(top, pltpu.roll(high, HALO, 0), low)
        extend(ext_ref, 2 * m)
        extend(ext_ref, 2 * m + 1)
        for n in range(2):
            for p in range(BY // 2):
                ends = ends_ref[2 * m + n, p].astype(F32)
                for i in range(2):
                    center_ref[2 * m + n, 2 * p + i, 0:HALO, :] = ends[8 * i : 8 * i + HALO]
                    center_ref[2 * m + n, 2 * p + i, HALO : HALO + 8, :] = jnp.zeros((8, 128), F32)
                    center_ref[2 * m + n, 2 * p + i, HALO + 8 :, :] = ends[8 * i + HALO : 8 * i + 8]
        return carry

    lax.fori_loop(0, total // 2, place, 0, unroll=2)

    def plane(c, carry):
        def center_of(m, dx):
            return center_ref[m, c, HALO - dx : HALO + 8 - dx, :] + center_ref[m, c, HALO + dx : HALO + 8 + dx, :]

        pair_sums(center_of, ext_ref, out_ref, scale, c, 0, EDGE_POINTS)
        return carry

    lax.fori_loop(0, BY, plane, 0)


def block_hot(tail):
    return jnp.where((iota((256, 128), 0) + 1).astype(F32) == tail[12:13, :], 1.0, 0.0).astype(BF16)


def spread_kernel(recv_ref, after_ref, out_ref, low_ref, high_ref, g_ref, h_ref):
    n_tiles = recv_ref.shape[0]

    group = 8

    def sources(g, total):
        for j in range(group):
            at = slice(j * 128, (j + 1) * 128)
            w = recv_ref[g * group + j, 0:TAIL, :].astype(F32)
            tail = recv_ref[g * group + j, TAIL:ROWS, :].astype(F32)
            h_ref[:, at] = block_hot(tail)
            for l in range(2):
                for k in range(MODES):
                    row = l * 128 + k * 32
                    g_ref[row : row + 32, at] = (w[l * 32 : l * 32 + 32, :] * tail[k : k + 1, :]).astype(BF16)
        return total + matmul(g_ref[...], h_ref[...], NT)

    r = lax.fori_loop(0, n_tiles // group, sources, jnp.zeros((256, 256), F32), unroll=2)
    for i in range(4):
        t = jnp.concatenate([r[0:128, i * 64 : i * 64 + 64], r[128:256, i * 64 : i * 64 + 64]], axis=1)
        if i == 0:
            low_ref[...] = t
        if i == 3:
            high_ref[...] = t
        for n in range(MODES * BY):
            out_ref[n, i * 4 : i * 4 + 4, :] = t[n * 4 : n * 4 + 4, :]


def image_kernel(recv_ref, f_ref, low_ref, high_ref, behind_ref, ahead_ref, ce_ref, out_ref, ext_ref, side_ref, q_ref, t_ref):
    n_tiles = recv_ref.shape[0]
    rows = f_ref.shape[1]
    for k in range(MODES):
        for c in range(BY):
            n = k * BY + c
            ext_ref[k, HALO + c] = f_ref[n]
            side_ref[k, HALO + c, 0:HALO, :] = high_ref[n * 4 : n * 4 + 4, :]
            side_ref[k, HALO + c, HALO:8, :] = low_ref[n * 4 : n * 4 + 4, :]
        extend(ext_ref, k)
        extend(side_ref, k)

    def weigh(ref, v, c, points, weights):
        sums = [{} for _ in range(MODES)]
        for dx, dy, n, i in points:
            weight = weights(i)[c, v * 8 : v * 8 + 8, :]
            for k in range(MODES):
                term = weight * ref[k, HALO + c + dy, v * 8 : v * 8 + 8, :]
                sums[k][dx] = sums[k][dx] + term if dx in sums[k] else term
        return sums

    def plane(cp, carry):
        for j in range(2):
            c = 2 * cp + j
            for v in range(rows // 8):
                for k, sums in enumerate(weigh(ext_ref, v, c, POINTS, lambda i: behind_ref.at[i] if i < CUT else ahead_ref.at[i - CUT])):
                    for dx, q in sums.items():
                        q_ref[k, j, dx + HALO, 8 + v * 8 : 16 + v * 8, :] = q
            for k, sums in enumerate(weigh(side_ref, 0, c, EDGE_POINTS, lambda i: ce_ref.at[i])):
                for dx, q in sums.items():
                    q_ref[k, j, HALO - dx, 0:8, :] = q
                    q_ref[k, j, HALO + dx, rows + 8 : rows + 16, :] = q
        for k in range(MODES):
            for i in range(4):
                both = []
                for j in range(2):
                    at = 8 + i * 4
                    v = q_ref[k, j, HALO, at : at + 4, :]
                    for dx in range(-HALO, HALO + 1):
                        if dx != 0:
                            v = v + q_ref[k, j, dx + HALO, at + dx : at + dx + 4, :]
                    both.append(v)
                row = pl.multiple_of(k * 32 + cp * 8, 8)
                t_ref[i, pl.ds(row, 8), :] = jnp.concatenate(both, axis=0)
        return carry

    lax.fori_loop(0, BY // 2, plane, 0)
    cov = jnp.concatenate(
        [
            jnp.concatenate([t_ref[i, :, l * 64 : l * 64 + 64] for i in range(4)], axis=1)
            for l in range(2)
        ],
        axis=0,
    )
    hi = cov.astype(BF16)
    lo = (cov - hi.astype(F32)).astype(BF16)
    both = jnp.concatenate([hi, lo], axis=0)
    group = 8

    def image(g, carry):
        cross, square = carry
        hots = [block_hot(recv_ref[g * group + j, TAIL:ROWS, :].astype(F32)) for j in range(group)]
        picked = matmul(both, jnp.concatenate(hots, axis=1), NN)
        picked = picked[0:256] + picked[256:512]
        for j in range(group):
            s = g * group + j
            w = recv_ref[s, 0:TAIL, :].astype(F32)
            tail = recv_ref[s, TAIL:ROWS, :].astype(F32)
            first = (j % 2) * 4
            pair = g * (group // 2) + j // 2
            for k in range(MODES):
                part = picked[k * 32 : k * 32 + 32, j * 128 : (j + 1) * 128] * w[0:32]
                part = part + picked[128 + k * 32 : 160 + k * 32, j * 128 : (j + 1) * 128] * w[32:64]
                out_ref[pair, first + k : first + k + 1, :] = jnp.sum(part, axis=0, keepdims=True)
            mode = tail[0:4] + tail[4:8] + tail[8:12]
            cross = cross + mode * out_ref[pair, first : first + 4, :]
            square = square + mode * mode
        return cross, square

    zero = jnp.zeros((MODES, 128), F32)
    cross, square = lax.fori_loop(0, n_tiles // group, image, (zero, zero), unroll=2)
    out_ref[n_tiles // 2, 0:4, :] = cross
    out_ref[n_tiles // 2, 4:8, :] = square


def gram_kernel(groups, parts_ref, other_ref, out_ref):
    n_tiles = out_ref.shape[0]
    pairs = n_tiles // 2
    sums = [jnp.zeros((8, 128), F32) for _ in range(MODES)]
    lane = iota((4, 128), 1)
    for p in range(pairs):
        z = parts_ref[p] + other_ref[p]
        out_ref[2 * p, 0:4, :] = z[0:4]
        out_ref[2 * p + 1, 0:4, :] = z[4:8]
        for d in range(MODES):
            sums[d] = sums[d] + z * (z if d == 0 else pltpu.roll(z, d, 0))
    last = parts_ref[pairs] + other_ref[pairs]
    stats = jnp.zeros((4, 128), F32)
    for d in range(MODES):
        both = sums[d][0:4] + sums[d][4:8]
        stats = jnp.where(lane == d, jnp.sum(both, axis=1, keepdims=True), stats)
    stats = jnp.where(lane == 4, jnp.sum(last[0:4], axis=1, keepdims=True), stats)
    stats = jnp.where(lane == 5, jnp.sum(last[4:8], axis=1, keepdims=True) * (1.0 / groups), stats)
    for s in range(n_tiles):
        out_ref[s, 4:8, :] = stats


def finish_kernel(back_ref, hot_ref, dest_ref, modes_ref, eigen_ref, rows_ref, split_ref):
    n_tiles = back_ref.shape[0]
    obs = dest_ref.shape[1]
    count = n_tiles * obs
    total = back_ref[0]
    for t in range(1, n_tiles):
        total = total + back_ref[t]

    def stat(k, lane):
        return total[4 + k : 5 + k, lane : lane + 1]

    def g(k, j):
        return stat(k, k - j) * (1.0 / count)

    low = {}
    for j in range(MODES):
        d = g(j, j)
        for p in range(j):
            d = d - low[j, p] * low[j, p]
        low[j, j] = jnp.sqrt(d)
        for k in range(j + 1, MODES):
            v = g(k, j)
            for p in range(j):
                v = v - low[k, p] * low[j, p]
            low[k, j] = v / low[j, j]
    rows = n_tiles * MODES
    for t in range(n_tiles):
        rows_ref[t * MODES : (t + 1) * MODES, :] = back_ref[t, 0:MODES, :]
    a = rows_ref[...]
    hi = a.astype(BF16)
    rest = a - hi.astype(F32)
    mid = rest.astype(BF16)
    split_ref[0:rows, :] = hi
    split_ref[rows : 2 * rows, :] = mid
    split_ref[2 * rows : 3 * rows, :] = (rest - mid.astype(F32)).astype(BF16)
    chunk = 1024
    second = iota((8, chunk), 0) >> 2

    def finish(c, carry):
        at = pl.ds(pl.multiple_of(c * chunk, chunk), chunk)
        r = matmul(split_ref[...], hot_ref[:, at], NN)
        r = (r[0:rows] + r[rows : 2 * rows]) + r[2 * rows : 3 * rows]
        dest = jnp.broadcast_to(dest_ref[:, at], (8, chunk)) - second
        image = jnp.zeros((8, chunk), F32)
        for t in range(0, n_tiles, 2):
            image = image + jnp.where(dest == t, r[t * MODES : t * MODES + 8], 0.0)
        image = image[0:MODES] + image[MODES:8]
        done = []
        for k in range(MODES):
            v = image[k : k + 1]
            for p in range(k):
                v = v - low[k, p] * done[p]
            done.append(v / low[k, k])
            modes_ref[k : k + 1, at] = done[k]
        return carry

    lax.fori_loop(0, obs // chunk, finish, 0, unroll=True)
    eigen = jnp.zeros((1, 128), F32)
    for k in range(MODES):
        eigen = jnp.where(iota((1, 128), 1) == k, stat(k, 4) / stat(k, 5), eigen)
    eigen_ref[...] = eigen[0, 0:MODES]


VM = pl.BlockSpec(memory_space=pltpu.VMEM)
SM = pl.BlockSpec(memory_space=pltpu.SMEM)
ANY = pl.BlockSpec(memory_space=pl.ANY)
HBM = pl.BlockSpec(memory_space=pltpu.HBM)


def struct(shape, dtype):
    return jax.ShapeDtypeStruct(shape, dtype)


def on_device(members, weights, modes_in, obs_tile, obs_block):
    n_tiles = lax.axis_size("tile")
    n_groups = lax.axis_size("mem")
    obs, width = weights.shape
    count, levels, rows, ny = members.shape
    half = lax.axis_index("mem") % 2
    dest = obs_tile.reshape(1, obs)
    block = obs_block.reshape(1, obs)

    with jax.named_scope("swap"):
        give = lax.dynamic_slice_in_dim(members, 2 - 2 * half, 2, axis=1)
        got = lax.ppermute(give, "mem", [(m, m ^ 1) for m in range(n_groups)])
    with jax.named_scope("pack"):
        sent, hot, keep = pl.pallas_call(
            pack_kernel,
            in_specs=[SM] + [HBM] * 5,
            out_specs=[VM] * 3,
            out_shape=[
                struct((n_tiles, ROWS, 128), BF16),
                struct((128, obs), BF16),
                struct((count, 2, rows, ny), BF16),
            ],
            scratch_shapes=[
                pltpu.VMEM((obs, width), BF16),
                pltpu.VMEM((MODES, obs), F32),
                pltpu.VMEM((1, obs), jnp.int32),
                pltpu.VMEM((1, obs), jnp.int32),
                pltpu.VMEM((ROWS, obs), BF16),
                pltpu.VMEM((16, obs), F32),
                pltpu.VMEM((8 * ROWS, obs), BF16),
                pltpu.VMEM((8 * ROWS, obs), BF16),
                pltpu.SemaphoreType.DMA((5,)),
            ],
            compiler_params=vmem(60),
        )(half.reshape(1), weights, modes_in, dest, block, members)
    with jax.named_scope("forward"):
        recv = lax.all_to_all(sent, "tile", 0, 0, tiled=True)
    up = [(t, (t + 1) % n_tiles) for t in range(n_tiles)]
    down = [(b, a) for a, b in up]

    with jax.named_scope("member_edges"):
        def edge(first):
            return jnp.concatenate([keep[:, :, first : first + HALO], got[:, :, first : first + HALO]], axis=0)

        first, last = edge(0), edge(rows - HALO)
        m_low = lax.ppermute(last, "tile", up)
        m_high = lax.ppermute(first, "tile", down)
    scale = 1.0 / (TOTAL * (count * n_groups - 1))
    with jax.named_scope("pairs"):
        behind, ahead, ends = pl.pallas_call(
            functools.partial(pair_kernel, scale),
            in_specs=[VM, VM],
            out_specs=[HBM, HBM, VM],
            out_shape=[
                struct((CUT, BY, rows, 128), F32),
                struct((len(POINTS) - CUT, BY, rows, 128), F32),
                struct((2 * count, BY // 2, 16, 128), BF16),
            ],
            scratch_shapes=[
                pltpu.VMEM((len(POINTS), BY, rows, 128), F32),
                pltpu.VMEM((2 * count, BY, rows + 16, 128), F32),
                pltpu.VMEM((2 * count, BY + 2 * HALO, rows, 128), F32),
                pltpu.VMEM((2 * count * 2 * rows, ny), F32),
                pltpu.SemaphoreType.DMA((2,)),
            ],
            compiler_params=pltpu.CompilerParams(vmem_limit_bytes=PAIRS_KIB << 10),
            cost_estimate=cost(8),
        )(keep, got)

    with jax.named_scope("spread"):
        field, f_low, f_high = pl.pallas_call(
            spread_kernel,
            in_specs=[VM, ANY],
            out_specs=[VM] * 3,
            out_shape=[
                struct((MODES * BY, rows, 128), F32),
                struct((128, 128), F32),
                struct((128, 128), F32),
            ],
            scratch_shapes=[
                pltpu.VMEM((256, 8 * 128), BF16),
                pltpu.VMEM((256, 8 * 128), BF16),
            ],
            compiler_params=vmem(),
        )(recv, ends)
    with jax.named_scope("spread_edges"):
        s_low = lax.ppermute(f_high, "tile", up)
        s_high = lax.ppermute(f_low, "tile", down)
    with jax.named_scope("pair_edges"):
        pairs_edge = pl.pallas_call(
            functools.partial(pair_edge_kernel, scale),
            in_specs=[VM, VM, VM, ANY],
            out_specs=VM,
            out_shape=struct((len(EDGE_POINTS), BY, 8, 128), F32),
            scratch_shapes=[
                pltpu.VMEM((2 * count, BY, 8 + 2 * HALO, 128), F32),
                pltpu.VMEM((2 * count, BY + 2 * HALO, 8, 128), F32),
                pltpu.VMEM((4 * 2 * count * HALO, ny), F32),
            ],
            compiler_params=vmem(6),
            cost_estimate=cost(3),
        )(ends, m_low, m_high, f_low)
    with jax.named_scope("images"):
        parts = pl.pallas_call(
            image_kernel,
            in_specs=[VM] * 7,
            out_specs=VM,
            out_shape=struct((n_tiles // 2 + 1, 8, 128), F32),
            scratch_shapes=[
                pltpu.VMEM((MODES, BY + 2 * HALO, rows, 128), F32),
                pltpu.VMEM((MODES, BY + 2 * HALO, 8, 128), F32),
                pltpu.VMEM((MODES, 2, 2 * HALO + 1, rows + 16, 128), F32),
                pltpu.VMEM((4, 128, 128), F32),
            ],
            compiler_params=vmem(),
        )(recv, field, s_low, s_high, behind, ahead, pairs_edge)
    with jax.named_scope("group_sum"):
        for step in (1, 3):
            parts = parts + lax.ppermute(parts, "mem", [(m, m ^ step) for m in range(n_groups)])
        other = lax.ppermute(parts, "mem", [(m, n_groups - 1 - m) for m in range(n_groups)])
    with jax.named_scope("gram"):
        back = pl.pallas_call(
            functools.partial(gram_kernel, n_groups),
            in_specs=[VM, VM],
            out_specs=VM,
            out_shape=struct((n_tiles, 8, 128), F32),
            compiler_params=vmem(4),
        )(parts, other)
    with jax.named_scope("return"):
        back = lax.all_to_all(back, "tile", 0, 0, tiled=True)
    with jax.named_scope("finish"):
        modes_out, eigen = pl.pallas_call(
            finish_kernel,
            in_specs=[VM] * 3,
            out_specs=[VM] * 2,
            out_shape=[struct((MODES, obs), F32), struct((MODES,), F32)],
            scratch_shapes=[
                pltpu.VMEM((n_tiles * MODES, 128), F32),
                pltpu.VMEM((3 * n_tiles * MODES, 128), BF16),
            ],
            compiler_params=vmem(),
        )(back, hot, dest)
    return modes_out, eigen


def solution(mesh):
    in_specs = (
        P("mem", None, "tile", None),
        P("tile", None),
        P(None, "tile"),
        P("tile", None),
        P("tile"),
    )
    out_specs = (P(None, "tile"), P())
    return jax.shard_map(
        on_device, mesh=mesh, in_specs=in_specs, out_specs=out_specs, check_vma=False
    )
```

```python
import functools

import jax
import jax.numpy as jnp
from jax import lax
from jax.experimental import pallas as pl
from jax.experimental.pallas import tpu as pltpu
from jax.sharding import PartitionSpec as P

BX = 4
BY = 8
STEPS = 4
MODES = 4
ROWS = 80
TAIL = 64
HALO = 4
F32 = jnp.float32
BF16 = jnp.bfloat16


def stencil_points():
    counts = {(0, 0): 1}
    for _ in range(STEPS):
        wider = {}
        for (dx, dy), n in counts.items():
            for sx, sy in ((0, 0), (1, 0), (-1, 0), (0, 1), (0, -1)):
                key = (dx + sx, dy + sy)
                wider[key] = wider.get(key, 0) + n
        counts = wider
    return sorted((dx, dy, n) for (dx, dy), n in counts.items())


POINTS = [(dx, dy, n, i) for i, (dx, dy, n) in enumerate(stencil_points())]
EDGE_POINTS = [p for p in POINTS if p[0] > 0]
EDGE_POINTS = [(dx, dy, n, i) for i, (dx, dy, n, _) in enumerate(EDGE_POINTS)]
TOTAL = float(5**STEPS)
CUT = len([p for p in POINTS if p[0] <= 0])

PAIRS_KIB = 65536 - 12000

NT = (((1,), (1,)), ((), ()))
NN = (((1,), (0,)), ((), ()))


def matmul(a, b, dims):
    return lax.dot_general(a, b, dims, preferred_element_type=F32)


def iota(shape, dim):
    return lax.broadcasted_iota(jnp.int32, shape, dim)


def cost(us):
    return pl.CostEstimate(flops=0, bytes_accessed=us * 3_690_000, transcendentals=0)


def vmem(limit=16):
    return pltpu.CompilerParams(vmem_limit_bytes=limit << 20)


def pack_kernel(
    half_ref, w_any, modes_any, dest_any, block_any, members_any, out_ref, hot_ref, keep_ref,
    w_ref, modes_ref, dest_ref, block_ref, x_ref, tail_ref, xa_ref, xb_ref, sems,
):
    n_tiles = out_ref.shape[0]
    obs = w_ref.shape[0]
    half = half_ref[0]
    pairs = (
        (dest_any, dest_ref),
        (w_any, w_ref),
        (modes_any, modes_ref),
        (block_any, block_ref),
        (members_any.at[:, pl.ds(2 * half, 2)], keep_ref),
    )
    copies = [pltpu.make_async_copy(a, b, sems.at[i]) for i, (a, b) in enumerate(pairs)]
    for copy in copies:
        copy.start()
    copies[0].wait()
    chunk = 256
    upper = jnp.where(iota((chunk, chunk), 0) < iota((chunk, chunk), 1), 1.0, 0.0).astype(BF16)
    off = jnp.zeros((n_tiles, 1), F32)
    for c in range(obs // chunk):
        at = slice(c * chunk, (c + 1) * chunk)
        d = jnp.where(iota((n_tiles, chunk), 0) == dest_ref[:, at], 1.0, 0.0)
        before = matmul(d.astype(BF16), upper, NN) + off
        rank = jnp.sum(d * before, axis=0, keepdims=True).astype(jnp.int32)
        hot_ref[:, at] = jnp.where(iota((128, chunk), 0) == rank, 1.0, 0.0).astype(BF16)
        off = off + jnp.sum(d, axis=1, keepdims=True)
    for copy in copies[1:]:
        copy.wait()
    q = iota((TAIL, 128), 0)
    source = (2 * half + (q >> 5)) * 32 + (q & 3) * 8 + ((q >> 2) & 7)
    order = jnp.where(iota((TAIL, 128), 1) == source, 1.0, 0.0).astype(BF16)
    x_ref[0:TAIL, :] = matmul(order, w_ref[...], NT).astype(BF16)
    m = modes_ref[...]
    hi = m.astype(BF16).astype(F32)
    mid = (m - hi).astype(BF16).astype(F32)
    lo = (m - hi) - mid
    tail_ref[0:4, :] = hi
    tail_ref[4:8, :] = mid
    tail_ref[8:12, :] = lo
    tail_ref[12:13, :] = (block_ref[...] + 1).astype(F32)
    tail_ref[13:16, :] = jnp.zeros((3, obs), F32)
    x_ref[TAIL:ROWS, :] = tail_ref[...].astype(BF16)
    group = 8
    rows = group * ROWS

    def send(g, carry):
        for part, xm_ref in enumerate((xa_ref, xb_ref)):
            first = (2 * g + part) * group
            for t in range(group):
                here = jnp.where(dest_ref[...] == first + t, 1.0, 0.0)
                here = jnp.broadcast_to(here, (16, obs)).astype(BF16)
                for r in range(ROWS // 16):
                    row = t * ROWS + r * 16
                    xm_ref[row : row + 16, :] = x_ref[r * 16 : r * 16 + 16, :] * here
            sent = matmul(xm_ref[...], hot_ref[...], NT)
            out_ref[pl.ds(first, group)] = sent.astype(BF16).reshape(group, ROWS, 128)
        return carry

    lax.fori_loop(0, n_tiles // (2 * group), send, 0, unroll=True)


def extend(ext_ref, lead):
    lane = iota((ext_ref.shape[-2], 128), 1) & 63
    for n in range(HALO):
        low = pltpu.roll(ext_ref[lead, HALO + BY - HALO + n], 1, 1)
        ext_ref[lead, n] = jnp.where(lane == 0, ext_ref[lead, HALO + HALO - 1 - n], low)
        high = pltpu.roll(ext_ref[lead, HALO + n], 127, 1)
        ext_ref[lead, HALO + BY + n] = jnp.where(lane == 63, ext_ref[lead, HALO + BY - 1 - n], high)


def spread_rows(x, move):
    return matmul(x, move, NN)


def mover(ny):
    lane = iota((ny, ny), 1)
    return jnp.where(iota((ny, ny), 0) == (lane & 63) * BY + (lane >> 6), 1.0, 0.0).astype(BF16)


def join(first, second, p):
    a = first[:, p * 128 : (p + 1) * 128]
    b = second[:, p * 128 : (p + 1) * 128]
    left = iota(a.shape, 1) < 64
    return jnp.where(left, a, pltpu.roll(b, 64, 1)), jnp.where(left, pltpu.roll(a, 64, 1), b)


def pair_sums(center_of, ext_ref, out_ref, scale, c, at, points):
    total = ext_ref.shape[0]

    def member(m, sums):
        ext = {dy: ext_ref[m, HALO + c + dy, at : at + 8, :] for _, dy, _, _ in points}
        center = {dx: center_of(m, dx) for dx, _, _, _ in points}
        return tuple(s + center[dx] * ext[dy] for s, (dx, dy, _, _) in zip(sums, points))

    sums = lax.fori_loop(
        0, total, member, tuple(jnp.zeros((8, 128), F32) for _ in points), unroll=10
    )
    for s, (dx, dy, n, i) in zip(sums, points):
        out_ref[i, c, at : at + 8, :] = s * (n * scale)


def pair_kernel(
    scale, keep_ref, got_ref, behind_any, ahead_any, ends_ref, out_ref, center_ref, ext_ref, y_ref, sems
):
    count = got_ref.shape[0]
    total = 2 * count
    rows = got_ref.shape[2]
    ny = got_ref.shape[3]
    move = mover(ny)
    side = count * 2 * rows
    for i, ref in enumerate((keep_ref, got_ref)):
        y_ref[i * side : (i + 1) * side, :] = spread_rows(ref[...].reshape(side, ny), move)

    def place(m, carry):
        row = pl.multiple_of(m * 2 * rows, 2 * rows)
        first = y_ref[pl.ds(row, rows), :]
        second = y_ref[pl.ds(row + rows, rows), :]
        zero = jnp.zeros((8, 128), F32)
        for p in range(BY // 2):
            both = join(first, second, p)
            ends = [both[0][rows - HALO :], both[0][0:HALO], both[1][rows - HALO :], both[1][0:HALO]]
            ends_ref[m, p] = jnp.concatenate(ends, axis=0).astype(BF16)
            for i, v in enumerate(both):
                c = 2 * p + i
                ext_ref[m, HALO + c] = v
                center_ref[m, c, 0:8, :] = zero
                center_ref[m, c, 8 : 8 + rows, :] = v
                center_ref[m, c, 8 + rows : 16 + rows, :] = zero
        extend(ext_ref, m)
        return carry

    lax.fori_loop(0, total, place, 0, unroll=4)

    def plane(c, carry):
        for v in range(rows // 8):

            def center_of(m, dx):
                return center_ref[m, c, 8 + v * 8 - dx : 16 + v * 8 - dx, :]

            pair_sums(center_of, ext_ref, out_ref, scale, c, v * 8, POINTS)
        pltpu.make_async_copy(out_ref.at[0:CUT, c], behind_any.at[:, c], sems.at[0]).start()
        pltpu.make_async_copy(out_ref.at[CUT:, c], ahead_any.at[:, c], sems.at[1]).start()
        return carry

    lax.fori_loop(0, BY, plane, 0)
    pltpu.make_async_copy(out_ref.at[0:CUT], behind_any, sems.at[0]).wait()
    pltpu.make_async_copy(out_ref.at[CUT:], ahead_any, sems.at[1]).wait()


def pair_edge_kernel(scale, ends_ref, low_ref, high_ref, after_ref, out_ref, center_ref, ext_ref, y_ref):
    total = center_ref.shape[0]
    ny = low_ref.shape[3]
    side = 2 * total * HALO
    move = mover(ny)
    for start, ref in ((0, high_ref), (side, low_ref)):
        rows = [ref[m, l].astype(F32) for l in range(2) for m in range(total)]
        y_ref[start : start + side, :] = spread_rows(jnp.concatenate(rows, axis=0).astype(BF16), move)

    def place(m, carry):
        blocks = []
        for start in (0, side):
            row = pl.multiple_of(start + m * 2 * HALO, 8)
            blocks.append((y_ref[pl.ds(row, 8), :], y_ref[pl.ds(row + side // 2, 8), :]))
        top = iota((8, 128), 0) < HALO
        for p in range(BY // 2):
            for i, (high, low) in enumerate(zip(join(*blocks[0], p), join(*blocks[1], p))):
                ext_ref[2 * m, HALO + 2 * p + i] = jnp.where(top, high, pltpu.roll(low, HALO, 0))
                ext_ref[2 * m + 1, HALO + 2 * p + i] = jnp.where(top, pltpu.roll(high, HALO, 0), low)
        extend(ext_ref, 2 * m)
        extend(ext_ref, 2 * m + 1)
        for n in range(2):
            for p in range(BY // 2):
                ends = ends_ref[2 * m + n, p].astype(F32)
                for i in range(2):
                    center_ref[2 * m + n, 2 * p + i, 0:HALO, :] = ends[8 * i : 8 * i + HALO]
                    center_ref[2 * m + n, 2 * p + i, HALO : HALO + 8, :] = jnp.zeros((8, 128), F32)
                    center_ref[2 * m + n, 2 * p + i, HALO + 8 :, :] = ends[8 * i + HALO : 8 * i + 8]
        return carry

    lax.fori_loop(0, total // 2, place, 0, unroll=2)

    def plane(c, carry):
        def center_of(m, dx):
            return center_ref[m, c, HALO - dx : HALO + 8 - dx, :] + center_ref[m, c, HALO + dx : HALO + 8 + dx, :]

        pair_sums(center_of, ext_ref, out_ref, scale, c, 0, EDGE_POINTS)
        return carry

    lax.fori_loop(0, BY, plane, 0)


def block_hot(tail):
    return jnp.where((iota((256, 128), 0) + 1).astype(F32) == tail[12:13, :], 1.0, 0.0).astype(BF16)


def spread_kernel(recv_ref, after_ref, out_ref, low_ref, high_ref, g_ref, h_ref):
    n_tiles = recv_ref.shape[0]

    group = 8

    def sources(g, total):
        for j in range(group):
            at = slice(j * 128, (j + 1) * 128)
            w = recv_ref[g * group + j, 0:TAIL, :].astype(F32)
            tail = recv_ref[g * group + j, TAIL:ROWS, :].astype(F32)
            h_ref[:, at] = block_hot(tail)
            for l in range(2):
                for k in range(MODES):
                    row = l * 128 + k * 32
                    g_ref[row : row + 32, at] = (w[l * 32 : l * 32 + 32, :] * tail[k : k + 1, :]).astype(BF16)
        return total + matmul(g_ref[...], h_ref[...], NT)

    r = lax.fori_loop(0, n_tiles // group, sources, jnp.zeros((256, 256), F32), unroll=True)
    for i in range(4):
        t = jnp.concatenate([r[0:128, i * 64 : i * 64 + 64], r[128:256, i * 64 : i * 64 + 64]], axis=1)
        if i == 0:
            low_ref[...] = t
        if i == 3:
            high_ref[...] = t
        for n in range(MODES * BY):
            out_ref[n, i * 4 : i * 4 + 4, :] = t[n * 4 : n * 4 + 4, :]


def image_kernel(recv_ref, f_ref, low_ref, high_ref, behind_ref, ahead_ref, ce_ref, out_ref, ext_ref, side_ref, q_ref, t_ref):
    n_tiles = recv_ref.shape[0]
    rows = f_ref.shape[1]
    for k in range(MODES):
        for c in range(BY):
            n = k * BY + c
            ext_ref[k, HALO + c] = f_ref[n]
            side_ref[k, HALO + c, 0:HALO, :] = high_ref[n * 4 : n * 4 + 4, :]
            side_ref[k, HALO + c, HALO:8, :] = low_ref[n * 4 : n * 4 + 4, :]
        extend(ext_ref, k)
        extend(side_ref, k)

    def weigh(ref, v, c, points, weights):
        sums = [{} for _ in range(MODES)]
        for dx, dy, n, i in points:
            weight = weights(i)[c, v * 8 : v * 8 + 8, :]
            for k in range(MODES):
                term = weight * ref[k, HALO + c + dy, v * 8 : v * 8 + 8, :]
                sums[k][dx] = sums[k][dx] + term if dx in sums[k] else term
        return sums

    def plane(cp, carry):
        for j in range(2):
            c = 2 * cp + j
            for v in range(rows // 8):
                for k, sums in enumerate(weigh(ext_ref, v, c, POINTS, lambda i: behind_ref.at[i] if i < CUT else ahead_ref.at[i - CUT])):
                    for dx, q in sums.items():
                        q_ref[k, j, dx + HALO, 8 + v * 8 : 16 + v * 8, :] = q
            for k, sums in enumerate(weigh(side_ref, 0, c, EDGE_POINTS, lambda i: ce_ref.at[i])):
                for dx, q in sums.items():
                    q_ref[k, j, HALO - dx, 0:8, :] = q
                    q_ref[k, j, HALO + dx, rows + 8 : rows + 16, :] = q
        for k in range(MODES):
            for i in range(4):
                both = []
                for j in range(2):
                    at = 8 + i * 4
                    v = q_ref[k, j, HALO, at : at + 4, :]
                    for dx in range(-HALO, HALO + 1):
                        if dx != 0:
                            v = v + q_ref[k, j, dx + HALO, at + dx : at + dx + 4, :]
                    both.append(v)
                row = pl.multiple_of(k * 32 + cp * 8, 8)
                t_ref[i, pl.ds(row, 8), :] = jnp.concatenate(both, axis=0)
        return carry

    lax.fori_loop(0, BY // 2, plane, 0)
    cov = jnp.concatenate(
        [
            jnp.concatenate([t_ref[i, :, l * 64 : l * 64 + 64] for i in range(4)], axis=1)
            for l in range(2)
        ],
        axis=0,
    )
    hi = cov.astype(BF16)
    lo = (cov - hi.astype(F32)).astype(BF16)
    both = jnp.concatenate([hi, lo], axis=0)
    group = 8

    def image(g, carry):
        cross, square = carry
        hots = [block_hot(recv_ref[g * group + j, TAIL:ROWS, :].astype(F32)) for j in range(group)]
        picked = matmul(both, jnp.concatenate(hots, axis=1), NN)
        picked = picked[0:256] + picked[256:512]
        for j in range(group):
            s = g * group + j
            w = recv_ref[s, 0:TAIL, :].astype(F32)
            tail = recv_ref[s, TAIL:ROWS, :].astype(F32)
            first = (j % 2) * 4
            pair = g * (group // 2) + j // 2
            for k in range(MODES):
                part = picked[k * 32 : k * 32 + 32, j * 128 : (j + 1) * 128] * w[0:32]
                part = part + picked[128 + k * 32 : 160 + k * 32, j * 128 : (j + 1) * 128] * w[32:64]
                out_ref[pair, first + k : first + k + 1, :] = jnp.sum(part, axis=0, keepdims=True)
            mode = tail[0:4] + tail[4:8] + tail[8:12]
            cross = cross + mode * out_ref[pair, first : first + 4, :]
            square = square + mode * mode
        return cross, square

    zero = jnp.zeros((MODES, 128), F32)
    cross, square = lax.fori_loop(0, n_tiles // group, image, (zero, zero), unroll=2)
    out_ref[n_tiles // 2, 0:4, :] = cross
    out_ref[n_tiles // 2, 4:8, :] = square


def gram_kernel(groups, parts_ref, other_ref, out_ref):
    n_tiles = out_ref.shape[0]
    pairs = n_tiles // 2
    sums = [jnp.zeros((8, 128), F32) for _ in range(MODES)]
    lane = iota((4, 128), 1)
    for p in range(pairs):
        z = parts_ref[p] + other_ref[p]
        out_ref[2 * p, 0:4, :] = z[0:4]
        out_ref[2 * p + 1, 0:4, :] = z[4:8]
        for d in range(MODES):
            sums[d] = sums[d] + z * (z if d == 0 else pltpu.roll(z, d, 0))
    last = parts_ref[pairs] + other_ref[pairs]
    stats = jnp.zeros((4, 128), F32)
    for d in range(MODES):
        both = sums[d][0:4] + sums[d][4:8]
        stats = jnp.where(lane == d, jnp.sum(both, axis=1, keepdims=True), stats)
    stats = jnp.where(lane == 4, jnp.sum(last[0:4], axis=1, keepdims=True), stats)
    stats = jnp.where(lane == 5, jnp.sum(last[4:8], axis=1, keepdims=True) * (1.0 / groups), stats)
    for s in range(n_tiles):
        out_ref[s, 4:8, :] = stats


def finish_kernel(back_ref, hot_ref, dest_ref, modes_ref, eigen_ref, rows_ref, split_ref):
    n_tiles = back_ref.shape[0]
    obs = dest_ref.shape[1]
    count = n_tiles * obs
    total = back_ref[0]
    for t in range(1, n_tiles):
        total = total + back_ref[t]

    def stat(k, lane):
        return total[4 + k : 5 + k, lane : lane + 1]

    def g(k, j):
        return stat(k, k - j) * (1.0 / count)

    low = {}
    for j in range(MODES):
        d = g(j, j)
        for p in range(j):
            d = d - low[j, p] * low[j, p]
        low[j, j] = jnp.sqrt(d)
        for k in range(j + 1, MODES):
            v = g(k, j)
            for p in range(j):
                v = v - low[k, p] * low[j, p]
            low[k, j] = v / low[j, j]
    rows = n_tiles * MODES
    for t in range(n_tiles):
        rows_ref[t * MODES : (t + 1) * MODES, :] = back_ref[t, 0:MODES, :]
    a = rows_ref[...]
    hi = a.astype(BF16)
    rest = a - hi.astype(F32)
    mid = rest.astype(BF16)
    split_ref[0:rows, :] = hi
    split_ref[rows : 2 * rows, :] = mid
    split_ref[2 * rows : 3 * rows, :] = (rest - mid.astype(F32)).astype(BF16)
    chunk = 1024
    second = iota((8, chunk), 0) >> 2

    def finish(c, carry):
        at = pl.ds(pl.multiple_of(c * chunk, chunk), chunk)
        r = matmul(split_ref[...], hot_ref[:, at], NN)
        r = (r[0:rows] + r[rows : 2 * rows]) + r[2 * rows : 3 * rows]
        dest = jnp.broadcast_to(dest_ref[:, at], (8, chunk)) - second
        image = jnp.zeros((8, chunk), F32)
        for t in range(0, n_tiles, 2):
            image = image + jnp.where(dest == t, r[t * MODES : t * MODES + 8], 0.0)
        image = image[0:MODES] + image[MODES:8]
        done = []
        for k in range(MODES):
            v = image[k : k + 1]
            for p in range(k):
                v = v - low[k, p] * done[p]
            done.append(v / low[k, k])
            modes_ref[k : k + 1, at] = done[k]
        return carry

    lax.fori_loop(0, obs // chunk, finish, 0, unroll=True)
    eigen = jnp.zeros((1, 128), F32)
    for k in range(MODES):
        eigen = jnp.where(iota((1, 128), 1) == k, stat(k, 4) / stat(k, 5), eigen)
    eigen_ref[...] = eigen[0, 0:MODES]


VM = pl.BlockSpec(memory_space=pltpu.VMEM)
SM = pl.BlockSpec(memory_space=pltpu.SMEM)
ANY = pl.BlockSpec(memory_space=pl.ANY)
HBM = pl.BlockSpec(memory_space=pltpu.HBM)


def struct(shape, dtype):
    return jax.ShapeDtypeStruct(shape, dtype)


def on_device(members, weights, modes_in, obs_tile, obs_block):
    n_tiles = lax.axis_size("tile")
    n_groups = lax.axis_size("mem")
    obs, width = weights.shape
    count, levels, rows, ny = members.shape
    half = lax.axis_index("mem") % 2
    dest = obs_tile.reshape(1, obs)
    block = obs_block.reshape(1, obs)

    with jax.named_scope("swap"):
        give = lax.dynamic_slice_in_dim(members, 2 - 2 * half, 2, axis=1)
        got = lax.ppermute(give, "mem", [(m, m ^ 1) for m in range(n_groups)])
    with jax.named_scope("pack"):
        sent, hot, keep = pl.pallas_call(
            pack_kernel,
            in_specs=[SM] + [HBM] * 5,
            out_specs=[VM] * 3,
            out_shape=[
                struct((n_tiles, ROWS, 128), BF16),
                struct((128, obs), BF16),
                struct((count, 2, rows, ny), BF16),
            ],
            scratch_shapes=[
                pltpu.VMEM((obs, width), BF16),
                pltpu.VMEM((MODES, obs), F32),
                pltpu.VMEM((1, obs), jnp.int32),
                pltpu.VMEM((1, obs), jnp.int32),
                pltpu.VMEM((ROWS, obs), BF16),
                pltpu.VMEM((16, obs), F32),
                pltpu.VMEM((8 * ROWS, obs), BF16),
                pltpu.VMEM((8 * ROWS, obs), BF16),
                pltpu.SemaphoreType.DMA((5,)),
            ],
            compiler_params=vmem(60),
        )(half.reshape(1), weights, modes_in, dest, block, members)
    with jax.named_scope("forward"):
        recv = lax.all_to_all(sent, "tile", 0, 0, tiled=True)
    up = [(t, (t + 1) % n_tiles) for t in range(n_tiles)]
    down = [(b, a) for a, b in up]

    with jax.named_scope("member_edges"):
        def edge(first):
            return jnp.concatenate([keep[:, :, first : first + HALO], got[:, :, first : first + HALO]], axis=0)

        first, last = edge(0), edge(rows - HALO)
        m_low = lax.ppermute(last, "tile", up)
        m_high = lax.ppermute(first, "tile", down)
    scale = 1.0 / (TOTAL * (count * n_groups - 1))
    with jax.named_scope("pairs"):
        behind, ahead, ends = pl.pallas_call(
            functools.partial(pair_kernel, scale),
            in_specs=[VM, VM],
            out_specs=[HBM, HBM, VM],
            out_shape=[
                struct((CUT, BY, rows, 128), F32),
                struct((len(POINTS) - CUT, BY, rows, 128), F32),
                struct((2 * count, BY // 2, 16, 128), BF16),
            ],
            scratch_shapes=[
                pltpu.VMEM((len(POINTS), BY, rows, 128), F32),
                pltpu.VMEM((2 * count, BY, rows + 16, 128), F32),
                pltpu.VMEM((2 * count, BY + 2 * HALO, rows, 128), F32),
                pltpu.VMEM((2 * count * 2 * rows, ny), F32),
                pltpu.SemaphoreType.DMA((2,)),
            ],
            compiler_params=pltpu.CompilerParams(vmem_limit_bytes=PAIRS_KIB << 10),
            cost_estimate=cost(8),
        )(keep, got)

    with jax.named_scope("spread"):
        field, f_low, f_high = pl.pallas_call(
            spread_kernel,
            in_specs=[VM, ANY],
            out_specs=[VM] * 3,
            out_shape=[
                struct((MODES * BY, rows, 128), F32),
                struct((128, 128), F32),
                struct((128, 128), F32),
            ],
            scratch_shapes=[
                pltpu.VMEM((256, 8 * 128), BF16),
                pltpu.VMEM((256, 8 * 128), BF16),
            ],
            compiler_params=vmem(),
        )(recv, ends)
    with jax.named_scope("spread_edges"):
        s_low = lax.ppermute(f_high, "tile", up)
        s_high = lax.ppermute(f_low, "tile", down)
    with jax.named_scope("pair_edges"):
        pairs_edge = pl.pallas_call(
            functools.partial(pair_edge_kernel, scale),
            in_specs=[VM, VM, VM, ANY],
            out_specs=VM,
            out_shape=struct((len(EDGE_POINTS), BY, 8, 128), F32),
            scratch_shapes=[
                pltpu.VMEM((2 * count, BY, 8 + 2 * HALO, 128), F32),
                pltpu.VMEM((2 * count, BY + 2 * HALO, 8, 128), F32),
                pltpu.VMEM((4 * 2 * count * HALO, ny), F32),
            ],
            compiler_params=vmem(6),
            cost_estimate=cost(3),
        )(ends, m_low, m_high, f_low)
    with jax.named_scope("images"):
        parts = pl.pallas_call(
            image_kernel,
            in_specs=[VM] * 7,
            out_specs=VM,
            out_shape=struct((n_tiles // 2 + 1, 8, 128), F32),
            scratch_shapes=[
                pltpu.VMEM((MODES, BY + 2 * HALO, rows, 128), F32),
                pltpu.VMEM((MODES, BY + 2 * HALO, 8, 128), F32),
                pltpu.VMEM((MODES, 2, 2 * HALO + 1, rows + 16, 128), F32),
                pltpu.VMEM((4, 128, 128), F32),
            ],
            compiler_params=vmem(),
        )(recv, field, s_low, s_high, behind, ahead, pairs_edge)
    with jax.named_scope("group_sum"):
        for step in (1, 3):
            parts = parts + lax.ppermute(parts, "mem", [(m, m ^ step) for m in range(n_groups)])
        other = lax.ppermute(parts, "mem", [(m, n_groups - 1 - m) for m in range(n_groups)])
    with jax.named_scope("gram"):
        back = pl.pallas_call(
            functools.partial(gram_kernel, n_groups),
            in_specs=[VM, VM],
            out_specs=VM,
            out_shape=struct((n_tiles, 8, 128), F32),
            compiler_params=vmem(4),
        )(parts, other)
    with jax.named_scope("return"):
        back = lax.all_to_all(back, "tile", 0, 0, tiled=True)
    with jax.named_scope("finish"):
        modes_out, eigen = pl.pallas_call(
            finish_kernel,
            in_specs=[VM] * 3,
            out_specs=[VM] * 2,
            out_shape=[struct((MODES, obs), F32), struct((MODES,), F32)],
            scratch_shapes=[
                pltpu.VMEM((n_tiles * MODES, 128), F32),
                pltpu.VMEM((3 * n_tiles * MODES, 128), BF16),
            ],
            compiler_params=vmem(),
        )(back, hot, dest)
    return modes_out, eigen


def solution(mesh):
    in_specs = (
        P("mem", None, "tile", None),
        P("tile", None),
        P(None, "tile"),
        P("tile", None),
        P("tile"),
    )
    out_specs = (P(None, "tile"), P())
    return jax.shard_map(
        on_device, mesh=mesh, in_specs=in_specs, out_specs=out_specs, check_vma=False
    )
```

```python
import functools

import jax
import jax.numpy as jnp
from jax import lax
from jax.experimental import pallas as pl
from jax.experimental.pallas import tpu as pltpu
from jax.sharding import PartitionSpec as P

BX = 4
BY = 8
STEPS = 4
MODES = 4
ROWS = 80
TAIL = 64
HALO = 4
F32 = jnp.float32
BF16 = jnp.bfloat16


def stencil_points():
    counts = {(0, 0): 1}
    for _ in range(STEPS):
        wider = {}
        for (dx, dy), n in counts.items():
            for sx, sy in ((0, 0), (1, 0), (-1, 0), (0, 1), (0, -1)):
                key = (dx + sx, dy + sy)
                wider[key] = wider.get(key, 0) + n
        counts = wider
    return sorted((dx, dy, n) for (dx, dy), n in counts.items())


POINTS = [(dx, dy, n, i) for i, (dx, dy, n) in enumerate(stencil_points())]
EDGE_POINTS = [p for p in POINTS if p[0] > 0]
EDGE_POINTS = [(dx, dy, n, i) for i, (dx, dy, n, _) in enumerate(EDGE_POINTS)]
TOTAL = float(5**STEPS)
CUT = len([p for p in POINTS if p[0] <= 0])

PAIRS_KIB = 65536 - 12000

NT = (((1,), (1,)), ((), ()))
NN = (((1,), (0,)), ((), ()))


def matmul(a, b, dims):
    return lax.dot_general(a, b, dims, preferred_element_type=F32)


def iota(shape, dim):
    return lax.broadcasted_iota(jnp.int32, shape, dim)


def cost(us):
    return pl.CostEstimate(flops=0, bytes_accessed=us * 3_690_000, transcendentals=0)


def vmem(limit=16):
    return pltpu.CompilerParams(vmem_limit_bytes=limit << 20)


def pack_kernel(
    half_ref, w_any, modes_any, dest_any, block_any, members_any, out_ref, hot_ref, keep_ref,
    w_ref, modes_ref, dest_ref, block_ref, x_ref, tail_ref, xa_ref, xb_ref, sems,
):
    n_tiles = out_ref.shape[0]
    obs = w_ref.shape[0]
    half = half_ref[0]
    pairs = (
        (dest_any, dest_ref),
        (w_any, w_ref),
        (modes_any, modes_ref),
        (block_any, block_ref),
        (members_any.at[:, pl.ds(2 * half, 2)], keep_ref),
    )
    copies = [pltpu.make_async_copy(a, b, sems.at[i]) for i, (a, b) in enumerate(pairs)]
    for copy in copies:
        copy.start()
    copies[0].wait()
    chunk = 256
    upper = jnp.where(iota((chunk, chunk), 0) < iota((chunk, chunk), 1), 1.0, 0.0).astype(BF16)
    off = jnp.zeros((n_tiles, 1), F32)
    for c in range(obs // chunk):
        at = slice(c * chunk, (c + 1) * chunk)
        d = jnp.where(iota((n_tiles, chunk), 0) == dest_ref[:, at], 1.0, 0.0)
        before = matmul(d.astype(BF16), upper, NN) + off
        rank = jnp.sum(d * before, axis=0, keepdims=True).astype(jnp.int32)
        hot_ref[:, at] = jnp.where(iota((128, chunk), 0) == rank, 1.0, 0.0).astype(BF16)
        off = off + jnp.sum(d, axis=1, keepdims=True)
    for copy in copies[1:]:
        copy.wait()
    q = iota((TAIL, 128), 0)
    source = (2 * half + (q >> 5)) * 32 + (q & 3) * 8 + ((q >> 2) & 7)
    order = jnp.where(iota((TAIL, 128), 1) == source, 1.0, 0.0).astype(BF16)
    x_ref[0:TAIL, :] = matmul(order, w_ref[...], NT).astype(BF16)
    m = modes_ref[...]
    hi = m.astype(BF16).astype(F32)
    mid = (m - hi).astype(BF16).astype(F32)
    lo = (m - hi) - mid
    tail_ref[0:4, :] = hi
    tail_ref[4:8, :] = mid
    tail_ref[8:12, :] = lo
    tail_ref[12:13, :] = (block_ref[...] + 1).astype(F32)
    tail_ref[13:16, :] = jnp.zeros((3, obs), F32)
    x_ref[TAIL:ROWS, :] = tail_ref[...].astype(BF16)
    group = 8
    rows = group * ROWS

    def send(g, carry):
        for part, xm_ref in enumerate((xa_ref, xb_ref)):
            first = (2 * g + part) * group
            for t in range(group):
                here = jnp.where(dest_ref[...] == first + t, 1.0, 0.0)
                here = jnp.broadcast_to(here, (16, obs)).astype(BF16)
                for r in range(ROWS // 16):
                    row = t * ROWS + r * 16
                    xm_ref[row : row + 16, :] = x_ref[r * 16 : r * 16 + 16, :] * here
            sent = matmul(xm_ref[...], hot_ref[...], NT)
            out_ref[pl.ds(first, group)] = sent.astype(BF16).reshape(group, ROWS, 128)
        return carry

    lax.fori_loop(0, n_tiles // (2 * group), send, 0, unroll=True)


def extend(ext_ref, lead):
    lane = iota((ext_ref.shape[-2], 128), 1) & 63
    for n in range(HALO):
        low = pltpu.roll(ext_ref[lead, HALO + BY - HALO + n], 1, 1)
        ext_ref[lead, n] = jnp.where(lane == 0, ext_ref[lead, HALO + HALO - 1 - n], low)
        high = pltpu.roll(ext_ref[lead, HALO + n], 127, 1)
        ext_ref[lead, HALO + BY + n] = jnp.where(lane == 63, ext_ref[lead, HALO + BY - 1 - n], high)


def spread_rows(x, move):
    return matmul(x, move, NN)


def mover(ny):
    lane = iota((ny, ny), 1)
    return jnp.where(iota((ny, ny), 0) == (lane & 63) * BY + (lane >> 6), 1.0, 0.0).astype(BF16)


def join(first, second, p):
    a = first[:, p * 128 : (p + 1) * 128]
    b = second[:, p * 128 : (p + 1) * 128]
    left = iota(a.shape, 1) < 64
    return jnp.where(left, a, pltpu.roll(b, 64, 1)), jnp.where(left, pltpu.roll(a, 64, 1), b)


def pair_sums(center_of, ext_ref, out_ref, scale, c, at, points):
    total = ext_ref.shape[0]

    def member(m, sums):
        ext = {dy: ext_ref[m, HALO + c + dy, at : at + 8, :] for _, dy, _, _ in points}
        center = {dx: center_of(m, dx) for dx, _, _, _ in points}
        return tuple(s + center[dx] * ext[dy] for s, (dx, dy, _, _) in zip(sums, points))

    sums = lax.fori_loop(
        0, total, member, tuple(jnp.zeros((8, 128), F32) for _ in points), unroll=10
    )
    for s, (dx, dy, n, i) in zip(sums, points):
        out_ref[i, c, at : at + 8, :] = s * (n * scale)


def pair_kernel(
    scale, keep_ref, got_ref, behind_any, ahead_any, ends_ref, out_ref, center_ref, ext_ref, y_ref, sems
):
    count = got_ref.shape[0]
    total = 2 * count
    rows = got_ref.shape[2]
    ny = got_ref.shape[3]
    move = mover(ny)
    side = count * 2 * rows
    for i, ref in enumerate((keep_ref, got_ref)):
        y_ref[i * side : (i + 1) * side, :] = spread_rows(ref[...].reshape(side, ny), move)

    def place(m, carry):
        row = pl.multiple_of(m * 2 * rows, 2 * rows)
        first = y_ref[pl.ds(row, rows), :]
        second = y_ref[pl.ds(row + rows, rows), :]
        zero = jnp.zeros((8, 128), F32)
        for p in range(BY // 2):
            both = join(first, second, p)
            ends = [both[0][rows - HALO :], both[0][0:HALO], both[1][rows - HALO :], both[1][0:HALO]]
            ends_ref[m, p] = jnp.concatenate(ends, axis=0).astype(BF16)
            for i, v in enumerate(both):
                c = 2 * p + i
                ext_ref[m, HALO + c] = v
                center_ref[m, c, 0:8, :] = zero
                center_ref[m, c, 8 : 8 + rows, :] = v
                center_ref[m, c, 8 + rows : 16 + rows, :] = zero
        extend(ext_ref, m)
        return carry

    lax.fori_loop(0, total, place, 0, unroll=4)

    def plane(c, carry):
        for v in range(rows // 8):

            def center_of(m, dx):
                return center_ref[m, c, 8 + v * 8 - dx : 16 + v * 8 - dx, :]

            pair_sums(center_of, ext_ref, out_ref, scale, c, v * 8, POINTS)
        pltpu.make_async_copy(out_ref.at[0:CUT, c], behind_any.at[:, c], sems.at[0]).start()
        pltpu.make_async_copy(out_ref.at[CUT:, c], ahead_any.at[:, c], sems.at[1]).start()
        return carry

    lax.fori_loop(0, BY, plane, 0)
    pltpu.make_async_copy(out_ref.at[0:CUT], behind_any, sems.at[0]).wait()
    pltpu.make_async_copy(out_ref.at[CUT:], ahead_any, sems.at[1]).wait()


def pair_edge_kernel(scale, ends_ref, low_ref, high_ref, after_ref, out_ref, center_ref, ext_ref, y_ref):
    total = center_ref.shape[0]
    ny = low_ref.shape[3]
    side = 2 * total * HALO
    move = mover(ny)
    for start, ref in ((0, high_ref), (side, low_ref)):
        rows = [ref[m, l].astype(F32) for l in range(2) for m in range(total)]
        y_ref[start : start + side, :] = spread_rows(jnp.concatenate(rows, axis=0).astype(BF16), move)

    def place(m, carry):
        blocks = []
        for start in (0, side):
            row = pl.multiple_of(start + m * 2 * HALO, 8)
            blocks.append((y_ref[pl.ds(row, 8), :], y_ref[pl.ds(row + side // 2, 8), :]))
        top = iota((8, 128), 0) < HALO
        for p in range(BY // 2):
            for i, (high, low) in enumerate(zip(join(*blocks[0], p), join(*blocks[1], p))):
                ext_ref[2 * m, HALO + 2 * p + i] = jnp.where(top, high, pltpu.roll(low, HALO, 0))
                ext_ref[2 * m + 1, HALO + 2 * p + i] = jnp.where(top, pltpu.roll(high, HALO, 0), low)
        extend(ext_ref, 2 * m)
        extend(ext_ref, 2 * m + 1)
        for n in range(2):
            for p in range(BY // 2):
                ends = ends_ref[2 * m + n, p].astype(F32)
                for i in range(2):
                    center_ref[2 * m + n, 2 * p + i, 0:HALO, :] = ends[8 * i : 8 * i + HALO]
                    center_ref[2 * m + n, 2 * p + i, HALO : HALO + 8, :] = jnp.zeros((8, 128), F32)
                    center_ref[2 * m + n, 2 * p + i, HALO + 8 :, :] = ends[8 * i + HALO : 8 * i + 8]
        return carry

    lax.fori_loop(0, total // 2, place, 0, unroll=2)

    def plane(c, carry):
        def center_of(m, dx):
            return center_ref[m, c, HALO - dx : HALO + 8 - dx, :] + center_ref[m, c, HALO + dx : HALO + 8 + dx, :]

        pair_sums(center_of, ext_ref, out_ref, scale, c, 0, EDGE_POINTS)
        return carry

    lax.fori_loop(0, BY, plane, 0)


def block_hot(tail):
    return jnp.where((iota((256, 128), 0) + 1).astype(F32) == tail[12:13, :], 1.0, 0.0).astype(BF16)


def spread_kernel(recv_ref, after_ref, out_ref, low_ref, high_ref, g_ref, h_ref):
    n_tiles = recv_ref.shape[0]

    group = 8

    def sources(g, total):
        for j in range(group):
            at = slice(j * 128, (j + 1) * 128)
            w = recv_ref[g * group + j, 0:TAIL, :].astype(F32)
            tail = recv_ref[g * group + j, TAIL:ROWS, :].astype(F32)
            h_ref[:, at] = block_hot(tail)
            for l in range(2):
                for k in range(MODES):
                    row = l * 128 + k * 32
                    g_ref[row : row + 32, at] = (w[l * 32 : l * 32 + 32, :] * tail[k : k + 1, :]).astype(BF16)
        return total + matmul(g_ref[...], h_ref[...], NT)

    r = lax.fori_loop(0, n_tiles // group, sources, jnp.zeros((256, 256), F32), unroll=True)
    for i in range(4):
        t = jnp.concatenate([r[0:128, i * 64 : i * 64 + 64], r[128:256, i * 64 : i * 64 + 64]], axis=1)
        if i == 0:
            low_ref[...] = t
        if i == 3:
            high_ref[...] = t
        for n in range(MODES * BY):
            out_ref[n, i * 4 : i * 4 + 4, :] = t[n * 4 : n * 4 + 4, :]


def image_kernel(recv_ref, f_ref, low_ref, high_ref, behind_ref, ahead_ref, ce_ref, out_ref, ext_ref, side_ref, q_ref, t_ref):
    n_tiles = recv_ref.shape[0]
    rows = f_ref.shape[1]
    for k in range(MODES):
        for c in range(BY):
            n = k * BY + c
            ext_ref[k, HALO + c] = f_ref[n]
            side_ref[k, HALO + c, 0:HALO, :] = high_ref[n * 4 : n * 4 + 4, :]
            side_ref[k, HALO + c, HALO:8, :] = low_ref[n * 4 : n * 4 + 4, :]
        extend(ext_ref, k)
        extend(side_ref, k)

    def weigh(ref, v, c, points, weights):
        sums = [{} for _ in range(MODES)]
        for dx, dy, n, i in points:
            weight = weights(i)[c, v * 8 : v * 8 + 8, :]
            for k in range(MODES):
                term = weight * ref[k, HALO + c + dy, v * 8 : v * 8 + 8, :]
                sums[k][dx] = sums[k][dx] + term if dx in sums[k] else term
        return sums

    def plane(cp, carry):
        for j in range(2):
            c = 2 * cp + j
            for v in range(rows // 8):
                for k, sums in enumerate(weigh(ext_ref, v, c, POINTS, lambda i: behind_ref.at[i] if i < CUT else ahead_ref.at[i - CUT])):
                    for dx, q in sums.items():
                        q_ref[k, j, dx + HALO, 8 + v * 8 : 16 + v * 8, :] = q
            for k, sums in enumerate(weigh(side_ref, 0, c, EDGE_POINTS, lambda i: ce_ref.at[i])):
                for dx, q in sums.items():
                    q_ref[k, j, HALO - dx, 0:8, :] = q
                    q_ref[k, j, HALO + dx, rows + 8 : rows + 16, :] = q
        for k in range(MODES):
            for i in range(4):
                both = []
                for j in range(2):
                    at = 8 + i * 4
                    v = q_ref[k, j, HALO, at : at + 4, :]
                    for dx in range(-HALO, HALO + 1):
                        if dx != 0:
                            v = v + q_ref[k, j, dx + HALO, at + dx : at + dx + 4, :]
                    both.append(v)
                row = pl.multiple_of(k * 32 + cp * 8, 8)
                t_ref[i, pl.ds(row, 8), :] = jnp.concatenate(both, axis=0)
        return carry

    lax.fori_loop(0, BY // 2, plane, 0)
    cov = jnp.concatenate(
        [
            jnp.concatenate([t_ref[i, :, l * 64 : l * 64 + 64] for i in range(4)], axis=1)
            for l in range(2)
        ],
        axis=0,
    )
    hi = cov.astype(BF16)
    lo = (cov - hi.astype(F32)).astype(BF16)
    both = jnp.concatenate([hi, lo], axis=0)
    group = 8

    def image(g, carry):
        cross, square = carry
        hots = [block_hot(recv_ref[g * group + j, TAIL:ROWS, :].astype(F32)) for j in range(group)]
        picked = matmul(both, jnp.concatenate(hots, axis=1), NN)
        picked = picked[0:256] + picked[256:512]
        for j in range(group):
            s = g * group + j
            w = recv_ref[s, 0:TAIL, :].astype(F32)
            tail = recv_ref[s, TAIL:ROWS, :].astype(F32)
            first = (j % 2) * 4
            pair = g * (group // 2) + j // 2
            for k in range(MODES):
                part = picked[k * 32 : k * 32 + 32, j * 128 : (j + 1) * 128] * w[0:32]
                part = part + picked[128 + k * 32 : 160 + k * 32, j * 128 : (j + 1) * 128] * w[32:64]
                out_ref[pair, first + k : first + k + 1, :] = jnp.sum(part, axis=0, keepdims=True)
            mode = tail[0:4] + tail[4:8] + tail[8:12]
            cross = cross + mode * out_ref[pair, first : first + 4, :]
            square = square + mode * mode
        return cross, square

    zero = jnp.zeros((MODES, 128), F32)
    cross, square = lax.fori_loop(0, n_tiles // group, image, (zero, zero), unroll=True)
    out_ref[n_tiles // 2, 0:4, :] = cross
    out_ref[n_tiles // 2, 4:8, :] = square


def gram_kernel(groups, parts_ref, other_ref, out_ref):
    n_tiles = out_ref.shape[0]
    pairs = n_tiles // 2
    sums = [jnp.zeros((8, 128), F32) for _ in range(MODES)]
    lane = iota((4, 128), 1)
    for p in range(pairs):
        z = parts_ref[p] + other_ref[p]
        out_ref[2 * p, 0:4, :] = z[0:4]
        out_ref[2 * p + 1, 0:4, :] = z[4:8]
        for d in range(MODES):
            sums[d] = sums[d] + z * (z if d == 0 else pltpu.roll(z, d, 0))
    last = parts_ref[pairs] + other_ref[pairs]
    stats = jnp.zeros((4, 128), F32)
    for d in range(MODES):
        both = sums[d][0:4] + sums[d][4:8]
        stats = jnp.where(lane == d, jnp.sum(both, axis=1, keepdims=True), stats)
    stats = jnp.where(lane == 4, jnp.sum(last[0:4], axis=1, keepdims=True), stats)
    stats = jnp.where(lane == 5, jnp.sum(last[4:8], axis=1, keepdims=True) * (1.0 / groups), stats)
    for s in range(n_tiles):
        out_ref[s, 4:8, :] = stats


def finish_kernel(back_ref, hot_ref, dest_ref, modes_ref, eigen_ref, rows_ref, split_ref):
    n_tiles = back_ref.shape[0]
    obs = dest_ref.shape[1]
    count = n_tiles * obs
    total = back_ref[0]
    for t in range(1, n_tiles):
        total = total + back_ref[t]

    def stat(k, lane):
        return total[4 + k : 5 + k, lane : lane + 1]

    def g(k, j):
        return stat(k, k - j) * (1.0 / count)

    low = {}
    for j in range(MODES):
        d = g(j, j)
        for p in range(j):
            d = d - low[j, p] * low[j, p]
        low[j, j] = jnp.sqrt(d)
        for k in range(j + 1, MODES):
            v = g(k, j)
            for p in range(j):
                v = v - low[k, p] * low[j, p]
            low[k, j] = v / low[j, j]
    rows = n_tiles * MODES
    for t in range(n_tiles):
        rows_ref[t * MODES : (t + 1) * MODES, :] = back_ref[t, 0:MODES, :]
    a = rows_ref[...]
    hi = a.astype(BF16)
    rest = a - hi.astype(F32)
    mid = rest.astype(BF16)
    split_ref[0:rows, :] = hi
    split_ref[rows : 2 * rows, :] = mid
    split_ref[2 * rows : 3 * rows, :] = (rest - mid.astype(F32)).astype(BF16)
    chunk = 1024
    second = iota((8, chunk), 0) >> 2

    def finish(c, carry):
        at = pl.ds(pl.multiple_of(c * chunk, chunk), chunk)
        r = matmul(split_ref[...], hot_ref[:, at], NN)
        r = (r[0:rows] + r[rows : 2 * rows]) + r[2 * rows : 3 * rows]
        dest = jnp.broadcast_to(dest_ref[:, at], (8, chunk)) - second
        image = jnp.zeros((8, chunk), F32)
        for t in range(0, n_tiles, 2):
            image = image + jnp.where(dest == t, r[t * MODES : t * MODES + 8], 0.0)
        image = image[0:MODES] + image[MODES:8]
        done = []
        for k in range(MODES):
            v = image[k : k + 1]
            for p in range(k):
                v = v - low[k, p] * done[p]
            done.append(v / low[k, k])
            modes_ref[k : k + 1, at] = done[k]
        return carry

    lax.fori_loop(0, obs // chunk, finish, 0, unroll=True)
    eigen = jnp.zeros((1, 128), F32)
    for k in range(MODES):
        eigen = jnp.where(iota((1, 128), 1) == k, stat(k, 4) / stat(k, 5), eigen)
    eigen_ref[...] = eigen[0, 0:MODES]


VM = pl.BlockSpec(memory_space=pltpu.VMEM)
SM = pl.BlockSpec(memory_space=pltpu.SMEM)
ANY = pl.BlockSpec(memory_space=pl.ANY)
HBM = pl.BlockSpec(memory_space=pltpu.HBM)


def struct(shape, dtype):
    return jax.ShapeDtypeStruct(shape, dtype)


def on_device(members, weights, modes_in, obs_tile, obs_block):
    n_tiles = lax.axis_size("tile")
    n_groups = lax.axis_size("mem")
    obs, width = weights.shape
    count, levels, rows, ny = members.shape
    half = lax.axis_index("mem") % 2
    dest = obs_tile.reshape(1, obs)
    block = obs_block.reshape(1, obs)

    with jax.named_scope("swap"):
        give = lax.dynamic_slice_in_dim(members, 2 - 2 * half, 2, axis=1)
        got = lax.ppermute(give, "mem", [(m, m ^ 1) for m in range(n_groups)])
    with jax.named_scope("pack"):
        sent, hot, keep = pl.pallas_call(
            pack_kernel,
            in_specs=[SM] + [HBM] * 5,
            out_specs=[VM] * 3,
            out_shape=[
                struct((n_tiles, ROWS, 128), BF16),
                struct((128, obs), BF16),
                struct((count, 2, rows, ny), BF16),
            ],
            scratch_shapes=[
                pltpu.VMEM((obs, width), BF16),
                pltpu.VMEM((MODES, obs), F32),
                pltpu.VMEM((1, obs), jnp.int32),
                pltpu.VMEM((1, obs), jnp.int32),
                pltpu.VMEM((ROWS, obs), BF16),
                pltpu.VMEM((16, obs), F32),
                pltpu.VMEM((8 * ROWS, obs), BF16),
                pltpu.VMEM((8 * ROWS, obs), BF16),
                pltpu.SemaphoreType.DMA((5,)),
            ],
            compiler_params=vmem(60),
        )(half.reshape(1), weights, modes_in, dest, block, members)
    with jax.named_scope("forward"):
        recv = lax.all_to_all(sent, "tile", 0, 0, tiled=True)
    up = [(t, (t + 1) % n_tiles) for t in range(n_tiles)]
    down = [(b, a) for a, b in up]

    with jax.named_scope("member_edges"):
        def edge(first):
            return jnp.concatenate([keep[:, :, first : first + HALO], got[:, :, first : first + HALO]], axis=0)

        first, last = edge(0), edge(rows - HALO)
        m_low = lax.ppermute(last, "tile", up)
        m_high = lax.ppermute(first, "tile", down)
    scale = 1.0 / (TOTAL * (count * n_groups - 1))
    with jax.named_scope("pairs"):
        behind, ahead, ends = pl.pallas_call(
            functools.partial(pair_kernel, scale),
            in_specs=[VM, VM],
            out_specs=[HBM, HBM, VM],
            out_shape=[
                struct((CUT, BY, rows, 128), F32),
                struct((len(POINTS) - CUT, BY, rows, 128), F32),
                struct((2 * count, BY // 2, 16, 128), BF16),
            ],
            scratch_shapes=[
                pltpu.VMEM((len(POINTS), BY, rows, 128), F32),
                pltpu.VMEM((2 * count, BY, rows + 16, 128), F32),
                pltpu.VMEM((2 * count, BY + 2 * HALO, rows, 128), F32),
                pltpu.VMEM((2 * count * 2 * rows, ny), F32),
                pltpu.SemaphoreType.DMA((2,)),
            ],
            compiler_params=pltpu.CompilerParams(vmem_limit_bytes=PAIRS_KIB << 10),
            cost_estimate=cost(8),
        )(keep, got)

    with jax.named_scope("spread"):
        field, f_low, f_high = pl.pallas_call(
            spread_kernel,
            in_specs=[VM, ANY],
            out_specs=[VM] * 3,
            out_shape=[
                struct((MODES * BY, rows, 128), F32),
                struct((128, 128), F32),
                struct((128, 128), F32),
            ],
            scratch_shapes=[
                pltpu.VMEM((256, 8 * 128), BF16),
                pltpu.VMEM((256, 8 * 128), BF16),
            ],
            compiler_params=vmem(),
        )(recv, ends)
    with jax.named_scope("spread_edges"):
        s_low = lax.ppermute(f_high, "tile", up)
        s_high = lax.ppermute(f_low, "tile", down)
    with jax.named_scope("pair_edges"):
        pairs_edge = pl.pallas_call(
            functools.partial(pair_edge_kernel, scale),
            in_specs=[VM, VM, VM, ANY],
            out_specs=VM,
            out_shape=struct((len(EDGE_POINTS), BY, 8, 128), F32),
            scratch_shapes=[
                pltpu.VMEM((2 * count, BY, 8 + 2 * HALO, 128), F32),
                pltpu.VMEM((2 * count, BY + 2 * HALO, 8, 128), F32),
                pltpu.VMEM((4 * 2 * count * HALO, ny), F32),
            ],
            compiler_params=vmem(6),
            cost_estimate=cost(3),
        )(ends, m_low, m_high, f_low)
    with jax.named_scope("images"):
        parts = pl.pallas_call(
            image_kernel,
            in_specs=[VM] * 7,
            out_specs=VM,
            out_shape=struct((n_tiles // 2 + 1, 8, 128), F32),
            scratch_shapes=[
                pltpu.VMEM((MODES, BY + 2 * HALO, rows, 128), F32),
                pltpu.VMEM((MODES, BY + 2 * HALO, 8, 128), F32),
                pltpu.VMEM((MODES, 2, 2 * HALO + 1, rows + 16, 128), F32),
                pltpu.VMEM((4, 128, 128), F32),
            ],
            compiler_params=vmem(),
        )(recv, field, s_low, s_high, behind, ahead, pairs_edge)
    with jax.named_scope("group_sum"):
        for step in (1, 3):
            parts = parts + lax.ppermute(parts, "mem", [(m, m ^ step) for m in range(n_groups)])
        other = lax.ppermute(parts, "mem", [(m, n_groups - 1 - m) for m in range(n_groups)])
    with jax.named_scope("gram"):
        back = pl.pallas_call(
            functools.partial(gram_kernel, n_groups),
            in_specs=[VM, VM],
            out_specs=VM,
            out_shape=struct((n_tiles, 8, 128), F32),
            compiler_params=vmem(4),
        )(parts, other)
    with jax.named_scope("return"):
        back = lax.all_to_all(back, "tile", 0, 0, tiled=True)
    with jax.named_scope("finish"):
        modes_out, eigen = pl.pallas_call(
            finish_kernel,
            in_specs=[VM] * 3,
            out_specs=[VM] * 2,
            out_shape=[struct((MODES, obs), F32), struct((MODES,), F32)],
            scratch_shapes=[
                pltpu.VMEM((n_tiles * MODES, 128), F32),
                pltpu.VMEM((3 * n_tiles * MODES, 128), BF16),
            ],
            compiler_params=vmem(),
        )(back, hot, dest)
    return modes_out, eigen


def solution(mesh):
    in_specs = (
        P("mem", None, "tile", None),
        P("tile", None),
        P(None, "tile"),
        P("tile", None),
        P("tile"),
    )
    out_specs = (P(None, "tile"), P())
    return jax.shard_map(
        on_device, mesh=mesh, in_specs=in_specs, out_specs=out_specs, check_vma=False
    )
```
